32 devices in a mesh: xy: 8 (over z, y), gz: 4 (over x, core).
Axes of the slice: x: 2, y: 2, z: 4, core: 2. Of those that a mesh axis runs over, the one named last changes fastest.
Arguments:
- base_field: bfloat16 [132, 32, 32, 256], P(None, 'gz', 'xy'), may hold values from 0 to 2
- increments: bfloat16 [132, 262144], P(None, ('xy', 'gz')), may hold values from -6 to 6
- dest_tile: int32 [262144, 1], P(('xy', 'gz')), may hold values from 0 to 7; in each aligned block of 8192 rows (0 to 8191, 8192 to 16383, ...) at most 2048 rows name the same one
- dest_cell: int32 [262144], P(('xy', 'gz')), may hold values from 0 to 8191
- courant_x: bfloat16 [32, 32, 256], P('gz', 'xy'), may hold values from -0.23925781 to 0.23925781
- courant_y: bfloat16 [32, 32, 256], P('gz', 'xy'), may hold values from -0.23925781 to 0.23925781
- fall_courant: float32 [132, 32], replicated, may hold values from 0.001 to 280
Outputs:
- settled: bfloat16 [132, 32, 32, 256], P(None, 'gz', 'xy')
The draws below stay inside these ranges and needn't reach their ends.
Inputs may be any that keep to these rules, and one draw needn't show every extreme that they name: `dest_tile`: among the rows of one device, at most 2048 name the same tile; in every draw some device has exactly 2048 rows naming one tile.
All inputs are finite; a program needn't handle non-finite values.
Results may differ from the reference program's by a relative error of at most 0.0043.
Values may be sent and summed in bfloat16 or wider, within the bound.
A program may use at most 128 MiB of HBM per device.

```python
import math
import jax
import jax.numpy as jnp
import numpy as np
from jax import lax

SPECTRUM_BINS = 132
TX = 4
TY = 256
LZ = 8
RD = 8192
CAP = 2048
X = 32
VERTICAL_LEVELS = 32
ROWS = 262144
N_XY = 8
N_GZ = 4


def draw_fall_courant(key, part):
    velocity_random_key, level_random_key, gust_random_key, location_random_key = jax.random.split(jax.random.fold_in(key, 17), 4)
    lower_log = math.log(0.5)
    terminal_velocity = jnp.exp(jax.random.uniform(velocity_random_key, (SPECTRUM_BINS, 1), jnp.float32, lower_log, math.log(200.0)))
    speed_multiplier = jnp.exp(jax.random.uniform(level_random_key, (SPECTRUM_BINS, VERTICAL_LEVELS), jnp.float32, math.log(0.7), math.log(1.4)))
    gust_level_rows = jax.random.randint(location_random_key, (3,), 0, VERTICAL_LEVELS)
    gust_event_mask = jnp.any(lax.broadcasted_iota(jnp.int32, (VERTICAL_LEVELS, 3), 0) == gust_level_rows[None, :], axis=1)
    gust_event = jnp.exp(jax.random.uniform(gust_random_key, (SPECTRUM_BINS, VERTICAL_LEVELS), jnp.float32, math.log(0.004), math.log(0.01)))
    return terminal_velocity * speed_multiplier * jnp.where(gust_event_mask[None, :], gust_event, 1.0)


def with_ends(values, own_key, smallest, largest):
    dims = values.shape
    spot = [jax.random.randint(jax.random.fold_in(own_key, axis), (), 0, dims[axis]) for axis in range(len(dims))]
    values = values.at[tuple(spot)].set(smallest)
    longest = dims.index(max(dims))
    spot[longest] = (spot[longest] + 1) % dims[longest]
    return values.at[tuple(spot)].set(largest)


def levels(own_key, shape, cuts, least, high):
    factor_of = 1.0
    for position, parts in cuts:
        draws = jax.random.uniform(jax.random.fold_in(jax.random.fold_in(own_key, 6), position), (parts,), jnp.float32, least / len(cuts), high / len(cuts))
        factor_of = factor_of * jnp.repeat(jnp.exp(draws), shape[position] // parts).reshape((-1,) + (1,) * (len(shape) - 1 - position))
    return factor_of


def shared_out(own_key, own, number, rows, amount, top, most, lean):
    order = jax.random.permutation(own_key, amount)
    heavy_load, ordinary = shares(amount, rows * top, most, lean, True), shares(amount, rows * top, most, lean, False)
    places = jnp.arange(amount)

    def named(lengths, rotation):
        used = int((lengths > 0).sum())
        fixed = max(1, used // 4)
        moved = fixed + (places - fixed + rotation * (used - fixed)) % max(1, amount - fixed)
        return jnp.zeros((amount,), jnp.int32).at[order[jnp.where(places < fixed, places, moved)]].set(jnp.asarray(lengths, jnp.int32))

    lengths = jnp.where(number % 4 == 0, named(heavy_load, number // 4), named(ordinary, number - number // 4 - 1))
    mixed = jax.random.permutation(jax.random.fold_in(own, 3), amount)
    donor, taker = mixed[0:amount // 2 * 2:2], mixed[1:amount // 2 * 2:2]
    room = jnp.minimum(lengths[donor] - 1, most - lengths[taker]) // 2
    room = jnp.where((donor == order[0]) | (taker == order[0]) | (lengths[taker] == 0), 0, jnp.maximum(room, 0))
    moved = jax.random.randint(jax.random.fold_in(own, 4), (amount // 2,), 0, 1 << 20) % (room + 1)
    lengths = lengths.at[donor].add(-moved).at[taker].add(moved)
    items = jnp.searchsorted(jnp.cumsum(lengths), jnp.arange(rows * top), side="right").astype(jnp.int32)
    grid = items.reshape(top, rows).T
    grid = grid[jax.random.permutation(jax.random.fold_in(own, 1), rows)]
    rotation = jax.random.randint(jax.random.fold_in(own, 2), (rows, 1), 0, top)
    return jnp.take_along_axis(grid, (jnp.arange(top)[None, :] + rotation) % top, axis=1)


def shares(amount, total, reach, skew, full):
    portions = [(1 << 20) // math.isqrt(standing ** skew) + 1 for standing in range(1, amount + 1)]
    largest = reach if full else min(reach, max(-(-total // amount), total * portions[0] // sum(portions)))
    least = 1 if total - largest >= amount - 1 else 0
    given, rest = [largest] + [least] * (amount - 1), total - largest - least * (amount - 1)
    while rest > 0:
        movable = [i for i in range(1, amount) if given[i] < largest] or [i for i in range(1, amount) if given[i] < reach]
        whole, remaining = sum([portions[i] for i in movable]), rest
        for i in movable:
            extra = min(reach - given[i], max(1, remaining * portions[i] // whole), rest)
            given[i] = given[i] + extra
            rest = rest - extra
    return np.array(given)


def normal_values(own_key, dims, deviation, most, pieces=(), kind=jnp.bfloat16):
    drawn = jax.random.normal(own_key, dims, jnp.float32) * deviation
    if len(pieces) > 0:
        drawn = levels(own_key, dims, pieces, -0.22, 0.18) * drawn
    return jnp.clip(drawn, min=-most, max=most).astype(kind)


def setup_inputs(seed: int = 0) -> dict:
    splits = jax.random.split(jax.random.key(seed), 8)
    base_field = jnp.clip(2.0 * jax.random.uniform(splits[0], (SPECTRUM_BINS, VERTICAL_LEVELS, X, TY), jnp.float32) ** levels(splits[0], (SPECTRUM_BINS, VERTICAL_LEVELS, X, TY), ((1, 4), (2, 8)), -0.2, 0.2), 0.0, 2.0).astype(jnp.bfloat16)
    increments = normal_values(splits[1], (SPECTRUM_BINS, ROWS), 1.0, 6.0, ((1, 32),))
    dest_tile_keys = jax.random.split(jax.random.fold_in(splits[2], 1), ROWS // RD)
    dest_tile_turns = jax.random.permutation(jax.random.fold_in(splits[2], 3), ROWS // RD)
    dest_tile = jax.vmap(lambda own, number: shared_out(jax.random.fold_in(splits[2], 2), own, number, RD, N_XY, 1, CAP, 2))(dest_tile_keys, dest_tile_turns).reshape((ROWS, 1))
    dest_cell = with_ends(jax.random.randint(splits[3], (ROWS,), 0, LZ * TX * TY), jax.random.fold_in(splits[3], 1), 0, (LZ * TX * TY) - 1).astype(jnp.int32)
    courant_x = jnp.clip(jax.random.uniform(splits[4], (VERTICAL_LEVELS, X, TY), jnp.float32, -0.23925781, 0.23925781) * levels(splits[4], (VERTICAL_LEVELS, X, TY), ((0, 4), (1, 8)), -0.4, 0.0), -0.23925781, 0.23925781).astype(jnp.bfloat16)
    courant_y = jnp.clip(jax.random.uniform(splits[5], (VERTICAL_LEVELS, X, TY), jnp.float32, -0.23925781, 0.23925781) * levels(splits[5], (VERTICAL_LEVELS, X, TY), ((0, 4), (1, 8)), -0.4, 0.0), -0.23925781, 0.23925781).astype(jnp.bfloat16)
    fall_courant = draw_fall_courant(jax.random.fold_in(splits[7], 71), 0)
    return dict(base_field=base_field, increments=increments, dest_tile=dest_tile, dest_cell=dest_cell, courant_x=courant_x, courant_y=courant_y, fall_courant=fall_courant)


def reference(base_field, increments, dest_tile, dest_cell, courant_x, courant_y, fall_courant):
    row_total = increments.shape[1]
    slab_index = (jnp.arange(row_total, dtype=jnp.int32) // RD) % N_GZ
    cell_index = dest_cell.astype(jnp.int32)
    level_index = slab_index * LZ + cell_index // (TX * TY)
    x_index = dest_tile[:, 0].astype(jnp.int32) * TX + (cell_index // TY) % TX
    y_index = cell_index % TY
    flat_index = (level_index * X + x_index) * TY + y_index
    face_x = courant_x.astype(jnp.float32)
    face_y = courant_y.astype(jnp.float32)

    def per_component(operands):
        base_part, increment, fall_rates = operands
        summed = jnp.zeros((VERTICAL_LEVELS * X * TY,), jnp.float32).at[flat_index].add(increment.astype(jnp.float32))
        updated = (base_part.astype(jnp.float32) + summed.reshape(VERTICAL_LEVELS, X, TY)).astype(jnp.bfloat16)
        updated = lax.optimization_barrier(updated)
        current = updated.astype(jnp.float32)
        from_left = jnp.pad(current, ((0, 0), (1, 0), (0, 0)))[:, :-1, :]
        flux_west = jnp.maximum(face_x, 0.0) * from_left + jnp.minimum(face_x, 0.0) * current
        flux_west = flux_west.at[:, 0, :].set(jnp.zeros((VERTICAL_LEVELS, TY), jnp.float32))
        flux_east = jnp.pad(flux_west[:, 1:, :], ((0, 0), (0, 1), (0, 0)))
        from_below = jnp.pad(current, ((0, 0), (0, 0), (1, 0)))[:, :, :-1]
        flux_south = jnp.maximum(face_y, 0.0) * from_below + jnp.minimum(face_y, 0.0) * current
        flux_south = flux_south.at[:, :, 0].set(jnp.zeros((VERTICAL_LEVELS, X), jnp.float32))
        flux_north = jnp.pad(flux_south[:, :, 1:], ((0, 0), (0, 0), (0, 1)))
        advected = (current - (flux_east - flux_west) - (flux_north - flux_south)).astype(jnp.bfloat16)
        advected = lax.optimization_barrier(advected)
        advected = advected.astype(jnp.float32)

        def descend(inflow, operands_level):
            layer, courant = operands_level
            value = (layer + inflow) / (1.0 + courant)
            return courant * value, value

        start = jnp.zeros((X, TY), jnp.float32)
        unused, outputs = lax.scan(descend, start, (advected[::-1], fall_rates[::-1]))
        return outputs[::-1].astype(jnp.bfloat16)

    return lax.map(per_component, (base_field, increments, fall_courant))
```

```python
import functools

import jax
import jax.numpy as jnp
from jax import lax
from jax.experimental import pallas as pl
from jax.experimental.pallas import tpu as pltpu
from jax.sharding import PartitionSpec as P

MESH = pl.DeviceIdType.MESH
NT = (((1,), (1,)), ((), ()))
TAIL = 16


def one_hot(condition):
    return jnp.where(condition, 1.0, 0.0).astype(jnp.bfloat16)


def stages_of(body):
    parts = [(body, TAIL)]
    first = 0
    while first < body:
        rows = 16 if body - first <= 32 else 32
        parts.append((first, rows))
        first += rows
    return parts


def pack_kernel(
    peers, capacity, inc, tiles, cells, main_out, tail_out, packed, tails, places, starts, table, sem, out_sem
):
    comps, count = inc.shape
    body = comps // 16 * 16
    height = body + TAIL
    run, width = 128, 256
    lines = count // run
    half = capacity // 2

    def clear(tile, carry):
        packed[tile] = jnp.zeros(packed.shape[1:], packed.dtype)
        return carry

    lax.fori_loop(0, peers, clear, 0)

    ahead = one_hot(
        lax.broadcasted_iota(jnp.int32, (run, run), 0) <= lax.broadcasted_iota(jnp.int32, (run, run), 1)
    )
    every = jnp.ones((run, run), jnp.bfloat16)
    above = one_hot(
        lax.broadcasted_iota(jnp.int32, (lines, lines), 0)
        > lax.broadcasted_iota(jnp.int32, (lines, lines), 1)
    )
    lanes = lax.broadcasted_iota(jnp.int32, (lines, run), 1)
    bundle = min(8, peers)

    def rank(part, carry):
        place, start = carry
        for n in range(bundle):
            tile = part * bundle + n
            member = jnp.where(tiles[...] == tile, 1.0, 0.0)
            taken = member.astype(jnp.bfloat16)
            inside = jnp.dot(taken, ahead, preferred_element_type=jnp.float32)
            line = jnp.dot(taken, every, preferred_element_type=jnp.float32).astype(jnp.bfloat16)
            before = jnp.dot(above, line, preferred_element_type=jnp.float32)
            place = place + member * (inside + before - 1.0)
            start = start + jnp.where(lanes == tile, before, 0.0)
        return place, start

    zero = jnp.zeros((lines, run), jnp.float32)
    place, start = lax.fori_loop(0, peers // bundle, rank, (zero, zero))
    places[...] = place.astype(jnp.int32) % width
    starts[...] = start.astype(jnp.int32)
    copy = pltpu.make_async_copy(starts, table, sem)
    copy.start()
    copy.wait()

    window = lax.broadcasted_iota(jnp.int32, (width, width), 0)
    lane = lax.broadcasted_iota(jnp.int32, (16, width), 1)
    sub = lax.broadcasted_iota(jnp.int32, (8, width), 0)

    def pair(ref, block):
        return jnp.concatenate([ref[pl.ds(2 * block, 1)], ref[pl.ds(2 * block + 1, 1)]], axis=1)

    def step(block, carry):
        columns = pl.ds(pl.multiple_of(block * width, width), width)
        match = one_hot(window == pair(places, block))
        owner = pair(tiles, block)
        cell = pair(cells, block)
        extra = jnp.concatenate(
            [inc[body:comps, columns].astype(jnp.float32), jnp.zeros((8 - comps + body, width), jnp.float32)],
            axis=0,
        )
        extra = jnp.where(sub == 4, (cell % width).astype(jnp.float32), extra)
        extra = jnp.where(sub == 5, (cell // width).astype(jnp.float32), extra)
        extra = jnp.concatenate([extra, jnp.zeros((8, width), jnp.float32)], axis=0)
        rows = jnp.concatenate([inc[0:body, columns], extra.astype(jnp.bfloat16)], axis=0)

        def place_part(part, inner):
            first = part * bundle
            masked = jnp.concatenate(
                [rows * one_hot(owner == first + n) for n in range(bundle)], axis=0
            )
            moved = lax.dot_general(masked, match, NT, preferred_element_type=jnp.float32)
            for n in range(bundle):
                tile = first + n
                begin = table[2 * block, tile]
                chunk, low = begin // width, begin % width
                value = moved[n * height : (n + 1) * height].astype(jnp.bfloat16)
                now = one_hot(lane >= low)
                later = one_hot(lane < low)
                here = pl.ds(pl.multiple_of(chunk * width, width), width)
                there = pl.ds(pl.multiple_of(chunk * width + width, width), width)
                now = jnp.concatenate([now] * (height // 16), axis=0)
                later = jnp.concatenate([later] * (height // 16), axis=0)
                packed[tile, :, here] += value * now
                packed[tile, :, there] = value * later
            return inner

        lax.fori_loop(0, peers // bundle, place_part, 0)
        return carry

    lax.fori_loop(0, count // width, step, 0)

    def out_copy(tile):
        return pltpu.make_async_copy(
            packed.at[tile, 0:body, 0:capacity], main_out.at[tile], out_sem.at[tile]
        )

    def leave(tile, carry):
        out_copy(tile).start()
        left = packed[tile, body:height, 0:half].astype(jnp.float32)[0:8]
        right = packed[tile, body:height, half:capacity].astype(jnp.float32)[0:8]
        tails[tile] = jnp.concatenate([left, right], axis=0).astype(jnp.bfloat16)
        return carry

    lax.fori_loop(0, peers, leave, 0)
    copy = pltpu.make_async_copy(tails, tail_out, sem)
    copy.start()

    def left_all(tile, carry):
        out_copy(tile).wait()
        return carry

    lax.fori_loop(0, peers, left_all, 0)
    copy.wait()


def main_kernel(
    comps, ahead, packed, tails, base_in, cx, cy, fall, out, arrived, arrived_tail, cell_of, base, total,
    updated, advected, left, right, next_cx, flow, inflow, scale, gain, weight, face, send_sem, recv_sem,
    halo_send, halo_recv, face_send, face_recv, flow_send, flow_recv, own_sem,
):
    peers, body, capacity = packed.shape
    xcells, levels, height, width = updated.shape
    slabs = lax.axis_size("gz")
    me, slab = lax.axis_index("xy"), lax.axis_index("gz")
    has_prev, has_next = me > 0, me < peers - 1
    groups = xcells * levels
    stages = stages_of(body)
    half = capacity // 2

    own_main = pltpu.make_async_copy(packed.at[me], arrived.at[0], own_sem.at[0])
    own_tail = pltpu.make_async_copy(tails.at[me], arrived_tail.at[0], own_sem.at[1])
    base_copy = pltpu.make_async_copy(base_in, base, own_sem.at[2])
    own_tail.start()
    own_main.start()
    base_copy.start()

    barrier = pltpu.get_barrier_semaphore()

    def greet(step, carry):
        pl.semaphore_signal(
            barrier, inc=1, device_id=((me + step) % peers, slab), device_id_type=MESH
        )
        return carry

    lax.fori_loop(1, peers, greet, 0)
    for step in range(1, slabs):
        pl.semaphore_signal(
            barrier, inc=1, device_id=(me, (slab + step) % slabs), device_id_type=MESH
        )
    pl.semaphore_wait(barrier, peers - 1 + slabs - 1)

    def row_copy(number, step):
        first, rows = stages[number]
        target = (me + step) % peers
        if number == 0:
            source, landing = tails.at[target], arrived_tail.at[step]
        else:
            source = packed.at[target, pl.ds(first, rows)]
            landing = arrived.at[step, pl.ds(first, rows)]
        return pltpu.make_async_remote_copy(
            src_ref=source,
            dst_ref=landing,
            send_sem=send_sem.at[number, step],
            recv_sem=recv_sem.at[number, step],
            device_id=(target, slab),
            device_id_type=MESH,
        )

    def turn(order):
        away = order // 2
        return jnp.where(order % 2 == 0, peers // 2 + away, peers // 2 - 1 - away)

    def start_rows(number):
        def start(order, carry):
            row_copy(number, turn(order)).start()
            return carry

        lax.fori_loop(0, peers - 1, start, 0)

    for number in range(min(ahead, len(stages))):
        start_rows(number)

    face_to_prev = pltpu.make_async_remote_copy(
        src_ref=cx.at[0],
        dst_ref=next_cx,
        send_sem=face_send,
        recv_sem=face_recv,
        device_id=((me + peers - 1) % peers, slab),
        device_id_type=MESH,
    )

    @pl.when(has_prev)
    def _():
        face_to_prev.start()

    @pl.when(jnp.logical_not(has_prev))
    def _():
        left[...] = jnp.zeros_like(left)

    @pl.when(jnp.logical_not(has_next))
    def _():
        right[...] = jnp.zeros_like(right)
        next_cx[...] = jnp.zeros_like(next_cx)

    column = lax.broadcasted_iota(jnp.int32, (1, fall.shape[1]), 1)

    def along(values, at):
        picked = jnp.sum(jnp.where(column == at, values, 0.0), axis=1, keepdims=True)
        return jnp.broadcast_to(picked, (values.shape[0], 128))

    for first, rows, filled in ((0, body, body), (body, TAIL, comps - body)):
        rates = fall[first : first + filled]
        if filled < rows:
            rates = jnp.concatenate([rates, jnp.zeros((8 - filled, fall.shape[1]), jnp.float32)], axis=0)
            spare = jnp.zeros((rows - 8, 128), jnp.float32)
        divided = 1.0 / (1.0 + rates)
        kept = rates / (1.0 + rates)

        def put(ref, at, value):
            if filled < rows:
                value = jnp.concatenate([value, spare], axis=0)
            ref[at, first : first + rows] = value

        def coefficients(k, carry):
            put(scale, k, along(divided, slab * levels + k))
            put(gain, k, along(kept, slab * levels + k))
            return carry

        lax.fori_loop(0, levels, coefficients, 0)
        passed = jnp.ones((kept.shape[0], 128), jnp.float32)
        put(weight, 0, passed)
        for d in range(1, slabs - 1):

            def through(k, value):
                return value * along(kept, (slab + d) * levels + k)

            passed = lax.fori_loop(0, levels, through, passed)
            put(weight, d, passed)

    lane_cells = lax.broadcasted_iota(jnp.int32, (width, capacity), 0).astype(jnp.float32)

    def wide(value):
        return jnp.concatenate([value] * (width // 128), axis=1)

    def add_rows(number, step, begin):
        first, rows = stages[number]
        bundle = min(groups, 1024 // rows)
        if number == 0:
            block = arrived_tail[step].astype(jnp.float32)
            block = jnp.concatenate([block[0:8], block[8:16]], axis=1)
            cell_of[step] = block
            block = jnp.concatenate([block, jnp.zeros_like(block)], axis=0).astype(jnp.bfloat16)
        else:
            block = arrived[step, first : first + rows]
        low = cell_of[step, 4:5]
        high = cell_of[step, 5:6]
        match = one_hot(lane_cells == low)

        def product(part, inner):
            at = part * bundle
            masked = jnp.concatenate(
                [block * one_hot(high == (at + n).astype(jnp.float32)) for n in range(bundle)], axis=0
            )
            sums = lax.dot_general(masked, match, NT, preferred_element_type=jnp.float32)
            sums = sums.reshape(bundle, rows, width)
            if begin and number > 0:
                total[pl.ds(at, bundle), first : first + rows] = sums + base[
                    pl.ds(at, bundle), first : first + rows
                ].astype(jnp.float32)
            elif begin:
                total[pl.ds(at, bundle), first : first + rows] = sums
            else:
                total[pl.ds(at, bundle), first : first + rows] += sums
            return inner

        lax.fori_loop(0, groups // bundle, product, 0)

    def halo_copy(number, which):
        first, rows = stages[number]
        source = updated.at[xcells - 1 if which == 0 else 0, :, pl.ds(first, rows)]
        landing = (left if which == 0 else right).at[:, pl.ds(first, rows)]
        return pltpu.make_async_remote_copy(
            src_ref=source,
            dst_ref=landing,
            send_sem=halo_send.at[number, which],
            recv_sem=halo_recv.at[number, which],
            device_id=((me + (1 if which == 0 else peers - 1)) % peers, slab),
            device_id_type=MESH,
        )

    def finish(number):
        first, rows = stages[number]
        span = slice(first, first + rows)

        def group(counter, carry):
            value = total[counter, span]
            if number == 0:
                value = jnp.concatenate(
                    [
                        value[: comps - body] + base[counter, body:comps].astype(jnp.float32),
                        jnp.zeros((rows - comps + body, width), jnp.float32),
                    ],
                    axis=0,
                )
            updated[counter % xcells, counter // xcells, span] = value.astype(jnp.bfloat16)
            return carry

        lax.fori_loop(0, groups, group, 0, unroll=4)

        @pl.when(has_next)
        def _():
            halo_copy(number, 0).start()

        @pl.when(has_prev)
        def _():
            halo_copy(number, 1).start()

    def flow_copy(number, d):
        first, rows = stages[number]
        return pltpu.make_async_remote_copy(
            src_ref=flow.at[:, pl.ds(first, rows)],
            dst_ref=inflow.at[d - 1, :, pl.ds(first, rows)],
            send_sem=flow_send.at[number, d - 1],
            recv_sem=flow_recv.at[number, d - 1],
            device_id=(me, (slab + slabs - d) % slabs),
            device_id_type=MESH,
        )

    def faces():
        @pl.when(has_next)
        def _():
            face_to_prev.wait_recv()

        for i in range(xcells):
            west, south = cx[i], cy[i]
            east = next_cx[...] if i == xcells - 1 else cx[i + 1]
            north = pltpu.roll(south, width - 1, 1)
            face[0, i] = (
                1.0
                - (jnp.maximum(east, 0.0) - jnp.minimum(west, 0.0))
                - (jnp.maximum(north, 0.0) - jnp.minimum(south, 0.0))
            )
            face[1, i] = jnp.maximum(west, 0.0)
            face[2, i] = -jnp.minimum(east, 0.0)
            face[3, i] = jnp.maximum(south, 0.0)
            face[4, i] = -jnp.minimum(north, 0.0)

    def spans(number):
        first, rows = stages[number]
        return [slice(at, at + 16) for at in range(first, first + rows, 16)]

    def advect(number):
        def cells(chosen, span):
            def level(counter, flows):
                k = levels - 1 - counter
                row = pl.ds(k, 1)
                wanted = sorted({i + d for i in chosen for d in (-1, 0, 1)})
                layer = {}
                for i in wanted:
                    ref = left[k, span] if i < 0 else right[k, span] if i == xcells else updated[i, k, span]
                    layer[i] = ref.astype(jnp.float32)
                kept = wide(gain[k, span])
                result = []
                for i, flowing in zip(chosen, flows):
                    current = layer[i]
                    value = (
                        current * face[0, i, row]
                        + layer[i - 1] * face[1, i, row]
                        + layer[i + 1] * face[2, i, row]
                        + pltpu.roll(current, 1, 1) * face[3, i, row]
                        + pltpu.roll(current, width - 1, 1) * face[4, i, row]
                    ).astype(jnp.bfloat16)
                    advected[i, k, span] = value
                    result.append((value.astype(jnp.float32) + flowing) * kept)
                return tuple(result)

            none = tuple(jnp.zeros((16, width), jnp.float32) for _ in chosen)
            flows = lax.fori_loop(0, levels, level, none, unroll=2)
            for i, flowing in zip(chosen, flows):
                flow[i, span] = flowing

        inner = list(range(1, xcells - 1))
        for span in spans(number):
            cells(inner, span)

        @pl.when(has_prev)
        def _():
            halo_copy(number, 0).wait_recv()

        @pl.when(has_next)
        def _():
            halo_copy(number, 1).wait_recv()

        for span in spans(number):
            cells([0, xcells - 1], span)
        for d in range(1, slabs):

            @pl.when(slab >= d)
            def _(d=d):
                flow_copy(number, d).start()

    def settle(number):
        @pl.when(slab == slabs - 1)
        def _():
            for i in range(xcells):
                for span in spans(number):
                    inflow[0, i, span] = jnp.zeros((16, width), jnp.float32)

        for d in range(1, slabs):

            @pl.when(slab + d < slabs)
            def _(d=d):
                flow_copy(number, d).wait_recv()
                if d > 1:
                    for i in range(xcells):
                        for span in spans(number):
                            inflow[0, i, span] += wide(weight[d - 1, span]) * inflow[d - 1, i, span]

        for span in spans(number):
            filled = min(comps, span.stop) - span.start

            def level(counter, flows):
                k = levels - 1 - counter
                kept, divided = wide(gain[k, span]), wide(scale[k, span])
                result = []
                for i, flowing in enumerate(flows):
                    value = advected[i, k, span].astype(jnp.float32) + flowing
                    done = (value * divided).astype(jnp.bfloat16)
                    out[k * xcells + i, span.start : span.start + filled] = done[:filled]
                    result.append(value * kept)
                return tuple(result)

            start = tuple(inflow[0, i, span] for i in range(xcells))
            lax.fori_loop(0, levels, level, start, unroll=2)

    own_tail.wait()
    faces()
    for number in range(len(stages)):
        if number + ahead < len(stages):
            start_rows(number + ahead)
        if number == 1:
            own_main.wait()
            base_copy.wait()
        add_rows(number, 0, True)
        if number == 1:
            finish(0)

        def receive(order, carry):
            step = turn(order)
            row_copy(number, step).wait_recv()
            add_rows(number, step, False)
            return carry

        middle = (peers - 1) // 2
        lax.fori_loop(0, middle, receive, 0)
        if number > 1:
            settle(number - 2)
        lax.fori_loop(middle, peers - 1, receive, 0)
        if number > 0:
            advect(number - 1)
        if number > 0:
            finish(number)
    settle(len(stages) - 2)
    advect(len(stages) - 1)
    settle(len(stages) - 1)

    for number in range(len(stages)):

        def sent(step, carry):
            row_copy(number, step).wait_send()
            return carry

        lax.fori_loop(1, peers, sent, 0)

        @pl.when(has_next)
        def _():
            halo_copy(number, 0).wait_send()

        @pl.when(has_prev)
        def _():
            halo_copy(number, 1).wait_send()

        for d in range(1, slabs):

            @pl.when(slab >= d)
            def _(d=d):
                flow_copy(number, d).wait_send()

    @pl.when(has_prev)
    def _():
        face_to_prev.wait_send()


def per_device(base_field, increments, dest_tile, dest_cell, courant_x, courant_y, fall_courant):
    comps, levels, xcells, ycells = base_field.shape
    row_count = increments.shape[1]
    peers, slabs = lax.axis_size("xy"), lax.axis_size("gz")
    capacity = 2 * row_count // peers
    body = comps // 16 * 16
    height = body + TAIL
    groups = levels * xcells
    count = len(stages_of(body))
    lines = row_count // 128

    vmem = pl.BlockSpec(memory_space=pltpu.VMEM)
    anywhere = pl.BlockSpec(memory_space=pl.ANY)
    packed, tails = pl.pallas_call(
        functools.partial(pack_kernel, peers, capacity),
        out_shape=(
            jax.ShapeDtypeStruct((peers, body, capacity), jnp.bfloat16),
            jax.ShapeDtypeStruct((peers, TAIL, capacity // 2), jnp.bfloat16),
        ),
        in_specs=[vmem] * 3,
        out_specs=(anywhere, anywhere),
        scratch_shapes=[
            pltpu.VMEM((peers, height, capacity + 256), jnp.bfloat16),
            pltpu.VMEM((peers, TAIL, capacity // 2), jnp.bfloat16),
            pltpu.VMEM((lines, 128), jnp.int32),
            pltpu.VMEM((lines, 128), jnp.int32),
            pltpu.SMEM((lines, 128), jnp.int32),
            pltpu.SemaphoreType.DMA,
            pltpu.SemaphoreType.DMA((peers,)),
        ],
        compiler_params=pltpu.CompilerParams(vmem_limit_bytes=48 * 2**20),
        name="pack_rows",
    )(increments, dest_tile.reshape(lines, 128), dest_cell.reshape(lines, 128))

    base = jnp.transpose(base_field, (1, 2, 0, 3)).reshape(groups, comps, ycells)
    first = jnp.logical_and(
        lax.axis_index("xy") == 0, jnp.arange(xcells)[:, None, None] == 0
    )
    face_x = jnp.where(first, 0.0, jnp.transpose(courant_x.astype(jnp.float32), (1, 0, 2)))
    face_y = jnp.transpose(courant_y.astype(jnp.float32), (1, 0, 2))
    face_y = jnp.where(jnp.arange(ycells)[None, None, :] == 0, 0.0, face_y)

    settled = pl.pallas_call(
        functools.partial(main_kernel, comps, 1),
        out_shape=jax.ShapeDtypeStruct((groups, comps, ycells), jnp.bfloat16),
        in_specs=[anywhere] * 3 + [vmem] * 3,
        out_specs=vmem,
        scratch_shapes=[
            pltpu.VMEM((peers, body, capacity), jnp.bfloat16),
            pltpu.VMEM((peers, TAIL, capacity // 2), jnp.bfloat16),
            pltpu.VMEM((peers, 8, capacity), jnp.float32),
            pltpu.VMEM((groups, comps, ycells), jnp.bfloat16),
            pltpu.VMEM((groups, height, ycells), jnp.float32),
            pltpu.VMEM((xcells, levels, height, ycells), jnp.bfloat16),
            pltpu.VMEM((xcells, levels, height, ycells), jnp.bfloat16),
            pltpu.VMEM((levels, height, ycells), jnp.bfloat16),
            pltpu.VMEM((levels, height, ycells), jnp.bfloat16),
            pltpu.VMEM((levels, ycells), jnp.float32),
            pltpu.VMEM((xcells, height, ycells), jnp.float32),
            pltpu.VMEM((slabs - 1, xcells, height, ycells), jnp.float32),
            pltpu.VMEM((levels, height, 128), jnp.float32),
            pltpu.VMEM((levels, height, 128), jnp.float32),
            pltpu.VMEM((slabs - 1, height, 128), jnp.float32),
            pltpu.VMEM((5, xcells, levels, ycells), jnp.float32),
            pltpu.SemaphoreType.DMA((count, peers)),
            pltpu.SemaphoreType.DMA((count, peers)),
            pltpu.SemaphoreType.DMA((count, 2)),
            pltpu.SemaphoreType.DMA((count, 2)),
            pltpu.SemaphoreType.DMA,
            pltpu.SemaphoreType.DMA,
            pltpu.SemaphoreType.DMA((count, slabs - 1)),
            pltpu.SemaphoreType.DMA((count, slabs - 1)),
            pltpu.SemaphoreType.DMA((3,)),
        ],
        compiler_params=pltpu.CompilerParams(
            vmem_limit_bytes=56 * 2**20, collective_id=0, has_side_effects=True
        ),
        name="exchange_advect_settle",
    )(packed, tails, base, face_x, face_y, fall_courant)
    settled = settled.reshape(levels, xcells, comps, ycells)
    return jnp.transpose(settled, (2, 0, 1, 3))


def solution(mesh):
    in_specs = (
        P(None, "gz", "xy", None),
        P(None, ("xy", "gz")),
        P(("xy", "gz"), None),
        P(("xy", "gz")),
        P("gz", "xy", None),
        P("gz", "xy", None),
        P(),
    )
    out_specs = P(None, "gz", "xy", None)
    return jax.shard_map(
        per_device, mesh=mesh, in_specs=in_specs, out_specs=out_specs, check_vma=False
    )
```

```python
import functools

import jax
import jax.numpy as jnp
from jax import lax
from jax.experimental import pallas as pl
from jax.experimental.pallas import tpu as pltpu
from jax.sharding import PartitionSpec as P

MESH = pl.DeviceIdType.MESH
NT = (((1,), (1,)), ((), ()))
TAIL = 16


def one_hot(condition):
    return jnp.where(condition, 1.0, 0.0).astype(jnp.bfloat16)


def stages_of(body):
    parts = [(body, TAIL)]
    first = 0
    while first < body:
        rows = 16 if body - first <= 32 else 32
        parts.append((first, rows))
        first += rows
    return parts


def pack_kernel(
    peers, capacity, inc_in, tiles, cells, main_out, tail_out, packed, tails, inc, places, starts, table, ends,
    totals, sem, out_sem
):
    comps, count = inc.shape
    inc_copy = pltpu.make_async_copy(inc_in, inc, out_sem.at[peers])
    inc_copy.start()
    body = comps // 16 * 16
    height = body + TAIL
    run, width = 128, 256
    lines = count // run
    half = capacity // 2

    def clear(tile, carry):
        packed[tile] = jnp.zeros(packed.shape[1:], packed.dtype)
        return carry

    lax.fori_loop(0, peers, clear, 0)

    ahead = one_hot(
        lax.broadcasted_iota(jnp.int32, (run, run), 0) <= lax.broadcasted_iota(jnp.int32, (run, run), 1)
    )
    every = jnp.ones((run, run), jnp.bfloat16)
    above = one_hot(
        lax.broadcasted_iota(jnp.int32, (lines, lines), 0)
        > lax.broadcasted_iota(jnp.int32, (lines, lines), 1)
    )
    lanes = lax.broadcasted_iota(jnp.int32, (lines, run), 1)
    bundle = min(8, peers)

    def rank(part, carry):
        place, start, end = carry
        for n in range(bundle):
            tile = part * bundle + n
            member = jnp.where(tiles[...] == tile, 1.0, 0.0)
            taken = member.astype(jnp.bfloat16)
            inside = jnp.dot(taken, ahead, preferred_element_type=jnp.float32)
            line = jnp.dot(taken, every, preferred_element_type=jnp.float32).astype(jnp.bfloat16)
            before = jnp.dot(above, line, preferred_element_type=jnp.float32)
            place = place + member * (inside + before - 1.0)
            start = start + jnp.where(lanes == tile, before, 0.0)
            end = end + jnp.where(
                lanes[0:8] == tile, before[lines - 1 : lines] + line[lines - 1 : lines].astype(jnp.float32), 0.0
            )
        return place, start, end

    zero = jnp.zeros((lines, run), jnp.float32)
    place, start, end = lax.fori_loop(0, peers // bundle, rank, (zero, zero, zero[0:8]))
    places[...] = place.astype(jnp.int32) % width
    starts[...] = start.astype(jnp.int32)
    ends[...] = end.astype(jnp.int32)
    copy = pltpu.make_async_copy(starts, table, sem)
    end_copy = pltpu.make_async_copy(ends, totals, out_sem.at[peers + 1])
    copy.start()
    end_copy.start()
    copy.wait()
    end_copy.wait()

    lane = lax.broadcasted_iota(jnp.int32, (16, width), 1)
    inc_copy.wait()

    def line_of(ref, line, much):
        return jnp.concatenate([ref[pl.ds(line + n, 1)] for n in range(much)], axis=1)

    def place_block(line, much):
        size = much * run
        columns = pl.ds(pl.multiple_of(line * run, run), size)
        window = lax.broadcasted_iota(jnp.int32, (width, size), 0)
        sub = lax.broadcasted_iota(jnp.int32, (8, size), 0)
        match = one_hot(window == line_of(places, line, much))
        owner = line_of(tiles, line, much)
        cell = line_of(cells, line, much)
        extra = jnp.concatenate(
            [inc[body:comps, columns].astype(jnp.float32), jnp.zeros((8 - comps + body, size), jnp.float32)],
            axis=0,
        )
        extra = jnp.where(sub == 4, (cell % width).astype(jnp.float32), extra)
        extra = jnp.where(sub == 5, (cell // width).astype(jnp.float32), extra)
        extra = jnp.concatenate([extra, jnp.zeros((8, size), jnp.float32)], axis=0)
        rows = jnp.concatenate([inc[0:body, columns], extra.astype(jnp.bfloat16)], axis=0)

        def place_part(part, inner):
            first = part * bundle
            masked = jnp.concatenate(
                [rows * one_hot(owner == first + n) for n in range(bundle)], axis=0
            )
            moved = lax.dot_general(masked, match, NT, preferred_element_type=jnp.float32)
            for n in range(bundle):
                tile = first + n
                begin = table[line, tile]
                chunk, low = begin // width, begin % width
                value = moved[n * height : (n + 1) * height].astype(jnp.bfloat16)
                now = one_hot(lane >= low)
                later = one_hot(lane < low)
                here = pl.ds(pl.multiple_of(chunk * width, width), width)
                there = pl.ds(pl.multiple_of(chunk * width + width, width), width)
                now = jnp.concatenate([now] * (height // 16), axis=0)
                later = jnp.concatenate([later] * (height // 16), axis=0)
                packed[tile, :, here] += value * now
                packed[tile, :, there] = value * later
            return inner

        lax.fori_loop(0, peers // bundle, place_part, 0)

    much = 4
    blocks = lines // much

    def step(block, carry):
        line = block * much
        following = jnp.minimum(line + much, lines - 1)

        def held(tile, most):
            end = jnp.where(block == blocks - 1, totals[0, tile], table[following, tile])
            return jnp.maximum(most, end - table[line, tile])

        most = lax.fori_loop(0, peers, held, 0, unroll=bundle)

        @pl.when(most <= width)
        def _():
            place_block(line, much)

        @pl.when(most > width)
        def _():
            def half_block(part, inner):
                place_block(line + 2 * part, 2)
                return inner

            lax.fori_loop(0, much // 2, half_block, 0)

        return carry

    lax.fori_loop(0, blocks, step, 0)

    def out_copy(tile):
        return pltpu.make_async_copy(
            packed.at[tile, 0:body, 0:capacity], main_out.at[tile], out_sem.at[tile]
        )

    def leave(tile, carry):
        out_copy(tile).start()
        left = packed[tile, body:height, 0:half].astype(jnp.float32)[0:8]
        right = packed[tile, body:height, half:capacity].astype(jnp.float32)[0:8]
        tails[tile] = jnp.concatenate([left, right], axis=0).astype(jnp.bfloat16)
        return carry

    lax.fori_loop(0, peers, leave, 0)
    copy = pltpu.make_async_copy(tails, tail_out, sem)
    copy.start()

    def left_all(tile, carry):
        out_copy(tile).wait()
        return carry

    lax.fori_loop(0, peers, left_all, 0)
    copy.wait()


def main_kernel(
    comps, ahead, packed, tails, base_in, courant_x, courant_y, fall_in, out, arrived, arrived_tail, cell_of, base, total,
    updated, advected, left, right, next_cx, flow, inflow, entry, scale, gain, weight, face, cx, cy, send_sem, recv_sem,
    halo_send, halo_recv, face_send, face_recv, flow_send, flow_recv, own_sem,
):
    peers, body, capacity = packed.shape
    xcells, levels, height, width = updated.shape
    slabs = lax.axis_size("gz")
    me, slab = lax.axis_index("xy"), lax.axis_index("gz")
    has_prev, has_next = me > 0, me < peers - 1
    groups = xcells * levels
    stages = stages_of(body)
    half = capacity // 2

    own_main = pltpu.make_async_copy(packed.at[me], arrived.at[0], own_sem.at[0])
    own_tail = pltpu.make_async_copy(tails.at[me], arrived_tail.at[0], own_sem.at[1])
    base_copy = pltpu.make_async_copy(base_in, base, own_sem.at[2])
    own_tail.start()
    own_main.start()
    base_copy.start()

    inner = (lax.broadcasted_iota(jnp.int32, (1, width), 1) > 0).astype(jnp.float32)
    for k in range(levels):
        along_x, along_y = courant_x[k].astype(jnp.float32), courant_y[k].astype(jnp.float32)
        for i in range(xcells):
            row = along_x[i : i + 1]
            cx[i, k : k + 1] = jnp.where(has_prev, row, 0.0) if i == 0 else row
            cy[i, k : k + 1] = along_y[i : i + 1] * inner

    barrier = pltpu.get_barrier_semaphore()

    def greet(step, carry):
        pl.semaphore_signal(
            barrier, inc=1, device_id=((me + step) % peers, slab), device_id_type=MESH
        )
        return carry

    lax.fori_loop(1, peers, greet, 0)
    for step in range(1, slabs):
        pl.semaphore_signal(
            barrier, inc=1, device_id=(me, (slab + step) % slabs), device_id_type=MESH
        )
    pl.semaphore_wait(barrier, peers - 1 + slabs - 1)

    def row_copy(number, step):
        first, rows = stages[number]
        target = (me + step) % peers
        if number == 0:
            source, landing = tails.at[target], arrived_tail.at[step]
        else:
            source = packed.at[target, pl.ds(first, rows)]
            landing = arrived.at[step, pl.ds(first, rows)]
        return pltpu.make_async_remote_copy(
            src_ref=source,
            dst_ref=landing,
            send_sem=send_sem.at[number, step],
            recv_sem=recv_sem.at[number, step],
            device_id=(target, slab),
            device_id_type=MESH,
        )

    def turn(order):
        away = order // 2
        return jnp.where(order % 2 == 0, peers // 2 + away, peers // 2 - 1 - away)

    def start_rows(number):
        def start(order, carry):
            row_copy(number, turn(order)).start()
            return carry

        lax.fori_loop(0, peers - 1, start, 0)

    for number in range(min(ahead, len(stages))):
        start_rows(number)

    face_to_prev = pltpu.make_async_remote_copy(
        src_ref=cx.at[0],
        dst_ref=next_cx,
        send_sem=face_send,
        recv_sem=face_recv,
        device_id=((me + peers - 1) % peers, slab),
        device_id_type=MESH,
    )

    @pl.when(has_prev)
    def _():
        face_to_prev.start()

    @pl.when(jnp.logical_not(has_prev))
    def _():
        left[...] = jnp.zeros_like(left)

    @pl.when(jnp.logical_not(has_next))
    def _():
        right[...] = jnp.zeros_like(right)
        next_cx[...] = jnp.zeros_like(next_cx)

    fall = jnp.transpose(fall_in[...])
    column = lax.broadcasted_iota(jnp.int32, (1, fall.shape[1]), 1)

    def along(values, at):
        picked = jnp.sum(jnp.where(column == at, values, 0.0), axis=1, keepdims=True)
        return jnp.broadcast_to(picked, (values.shape[0], 128))

    for first, rows, filled in ((0, body, body), (body, TAIL, comps - body)):
        rates = fall[first : first + filled]
        if filled < rows:
            rates = jnp.concatenate([rates, jnp.zeros((8 - filled, fall.shape[1]), jnp.float32)], axis=0)
            spare = jnp.zeros((rows - 8, 128), jnp.float32)
        divided = 1.0 / (1.0 + rates)
        kept = rates / (1.0 + rates)

        def put(ref, at, value):
            if filled < rows:
                value = jnp.concatenate([value, spare], axis=0)
            ref[at, first : first + rows] = value

        def coefficients(k, carry):
            put(scale, k, along(divided, slab * levels + k))
            put(gain, k, along(kept, slab * levels + k))
            return carry

        lax.fori_loop(0, levels, coefficients, 0)
        passed = jnp.ones((kept.shape[0], 128), jnp.float32)
        put(weight, 0, passed)
        for d in range(1, slabs - 1):

            def through(k, value):
                return value * along(kept, (slab + d) * levels + k)

            passed = lax.fori_loop(0, levels, through, passed)
            put(weight, d, passed)

    lane_cells = lax.broadcasted_iota(jnp.int32, (width, capacity), 0).astype(jnp.float32)

    def wide(value):
        return jnp.concatenate([value] * (width // 128), axis=1)

    def add_rows(number, step, begin):
        first, rows = stages[number]
        bundle = min(groups, 1024 // rows)
        if number == 0:
            block = arrived_tail[step].astype(jnp.float32)
            block = jnp.concatenate([block[0:8], block[8:16]], axis=1)
            cell_of[step] = block
            block = jnp.concatenate([block, jnp.zeros_like(block)], axis=0).astype(jnp.bfloat16)
        else:
            block = arrived[step, first : first + rows]
        low = cell_of[step, 4:5]
        high = cell_of[step, 5:6]
        match = one_hot(lane_cells == low)

        def product(part, inner):
            at = part * bundle
            masked = jnp.concatenate(
                [block * one_hot(high == (at + n).astype(jnp.float32)) for n in range(bundle)], axis=0
            )
            sums = lax.dot_general(masked, match, NT, preferred_element_type=jnp.float32)
            sums = sums.reshape(bundle, rows, width)
            if begin and number > 0:
                total[pl.ds(at, bundle), first : first + rows] = sums + base[
                    pl.ds(at, bundle), first : first + rows
                ].astype(jnp.float32)
            elif begin:
                total[pl.ds(at, bundle), first : first + rows] = sums
            else:
                total[pl.ds(at, bundle), first : first + rows] += sums
            return inner

        lax.fori_loop(0, groups // bundle, product, 0)

    def halo_copy(number, which):
        first, rows = stages[number]
        source = updated.at[xcells - 1 if which == 0 else 0, :, pl.ds(first, rows)]
        landing = (left if which == 0 else right).at[:, pl.ds(first, rows)]
        return pltpu.make_async_remote_copy(
            src_ref=source,
            dst_ref=landing,
            send_sem=halo_send.at[number, which],
            recv_sem=halo_recv.at[number, which],
            device_id=((me + (1 if which == 0 else peers - 1)) % peers, slab),
            device_id_type=MESH,
        )

    def finish(number):
        first, rows = stages[number]
        span = slice(first, first + rows)

        def group(counter, carry):
            value = total[counter, span]
            if number == 0:
                value = jnp.concatenate(
                    [
                        value[: comps - body] + base[counter, body:comps].astype(jnp.float32),
                        jnp.zeros((rows - comps + body, width), jnp.float32),
                    ],
                    axis=0,
                )
            updated[counter % xcells, counter // xcells, span] = value.astype(jnp.bfloat16)
            return carry

        lax.fori_loop(0, groups, group, 0, unroll=4)

        @pl.when(has_next)
        def _():
            halo_copy(number, 0).start()

        @pl.when(has_prev)
        def _():
            halo_copy(number, 1).start()

    def flow_copy(number, d):
        first, rows = stages[number]
        return pltpu.make_async_remote_copy(
            src_ref=flow.at[:, pl.ds(first, rows)],
            dst_ref=inflow.at[d - 1, :, pl.ds(first, rows)],
            send_sem=flow_send.at[number, d - 1],
            recv_sem=flow_recv.at[number, d - 1],
            device_id=(me, (slab + slabs - d) % slabs),
            device_id_type=MESH,
        )

    def faces():
        @pl.when(has_next)
        def _():
            face_to_prev.wait_recv()

        for i in range(xcells):
            west, south = cx[i], cy[i]
            east = next_cx[...] if i == xcells - 1 else cx[i + 1]
            north = pltpu.roll(south, width - 1, 1)
            face[0, i] = (
                1.0
                - (jnp.maximum(east, 0.0) - jnp.minimum(west, 0.0))
                - (jnp.maximum(north, 0.0) - jnp.minimum(south, 0.0))
            )
            face[1, i] = jnp.maximum(west, 0.0)
            face[2, i] = -jnp.minimum(east, 0.0)
            face[3, i] = jnp.maximum(south, 0.0)
            face[4, i] = -jnp.minimum(north, 0.0)

    def spans(number):
        first, rows = stages[number]
        return [slice(at, at + 16) for at in range(first, first + rows, 16)]

    def advect(number):
        def cells(chosen, span):
            def level(counter, flows):
                k = levels - 1 - counter
                row = pl.ds(k, 1)
                wanted = sorted({i + d for i in chosen for d in (-1, 0, 1)})
                layer = {}
                for i in wanted:
                    ref = left[k, span] if i < 0 else right[k, span] if i == xcells else updated[i, k, span]
                    layer[i] = ref.astype(jnp.float32)
                kept = wide(gain[k, span])
                result = []
                for i, flowing in zip(chosen, flows):
                    current = layer[i]
                    value = (
                        current * face[0, i, row]
                        + layer[i - 1] * face[1, i, row]
                        + layer[i + 1] * face[2, i, row]
                        + pltpu.roll(current, 1, 1) * face[3, i, row]
                        + pltpu.roll(current, width - 1, 1) * face[4, i, row]
                    ).astype(jnp.bfloat16)
                    advected[i, k, span] = value
                    result.append((value.astype(jnp.float32) + flowing) * kept)
                return tuple(result)

            none = tuple(jnp.zeros((16, width), jnp.float32) for _ in chosen)
            flows = lax.fori_loop(0, levels, level, none, unroll=2)
            for i, flowing in zip(chosen, flows):
                flow[i, span] = flowing.astype(jnp.bfloat16)

        inner = list(range(1, xcells - 1))
        for span in spans(number):
            cells(inner, span)

        @pl.when(has_prev)
        def _():
            halo_copy(number, 0).wait_recv()

        @pl.when(has_next)
        def _():
            halo_copy(number, 1).wait_recv()

        for span in spans(number):
            cells([0, xcells - 1], span)
        for d in range(1, slabs):

            @pl.when(slab >= d)
            def _(d=d):
                flow_copy(number, d).start()

    def settle(number):
        @pl.when(slab == slabs - 1)
        def _():
            for i in range(xcells):
                for span in spans(number):
                    entry[i, span] = jnp.zeros((16, width), jnp.float32)

        for d in range(1, slabs):

            @pl.when(slab + d < slabs)
            def _(d=d):
                flow_copy(number, d).wait_recv()
                for i in range(xcells):
                    for span in spans(number):
                        came = inflow[d - 1, i, span].astype(jnp.float32)
                        if d == 1:
                            entry[i, span] = came
                        else:
                            entry[i, span] += wide(weight[d - 1, span]) * came

        for span in spans(number):
            filled = min(comps, span.stop) - span.start

            def level(counter, flows):
                k = levels - 1 - counter
                kept, divided = wide(gain[k, span]), wide(scale[k, span])
                result = []
                for i, flowing in enumerate(flows):
                    value = advected[i, k, span].astype(jnp.float32) + flowing
                    done = (value * divided).astype(jnp.bfloat16)
                    out[k * xcells + i, span.start : span.start + filled] = done[:filled]
                    result.append(value * kept)
                return tuple(result)

            start = tuple(entry[i, span] for i in range(xcells))
            lax.fori_loop(0, levels, level, start, unroll=2)

    own_tail.wait()
    faces()
    for number in range(len(stages)):
        if number + ahead < len(stages):
            start_rows(number + ahead)
        if number == 1:
            own_main.wait()
            base_copy.wait()
        add_rows(number, 0, True)
        if number == 1:
            finish(0)

        def receive(order, carry):
            step = turn(order)
            row_copy(number, step).wait_recv()
            add_rows(number, step, False)
            return carry

        middle = (peers - 1) // 2
        lax.fori_loop(0, middle, receive, 0)
        if number > 1:
            settle(number - 2)
        lax.fori_loop(middle, peers - 1, receive, 0)
        if number > 0:
            advect(number - 1)
        if number > 0:
            finish(number)
    settle(len(stages) - 2)
    advect(len(stages) - 1)
    settle(len(stages) - 1)

    for number in range(len(stages)):

        def sent(step, carry):
            row_copy(number, step).wait_send()
            return carry

        lax.fori_loop(1, peers, sent, 0)

        @pl.when(has_next)
        def _():
            halo_copy(number, 0).wait_send()

        @pl.when(has_prev)
        def _():
            halo_copy(number, 1).wait_send()

        for d in range(1, slabs):

            @pl.when(slab >= d)
            def _(d=d):
                flow_copy(number, d).wait_send()

    @pl.when(has_prev)
    def _():
        face_to_prev.wait_send()


def per_device(base_field, increments, dest_tile, dest_cell, courant_x, courant_y, fall_courant):
    comps, levels, xcells, ycells = base_field.shape
    row_count = increments.shape[1]
    peers, slabs = lax.axis_size("xy"), lax.axis_size("gz")
    capacity = 2 * row_count // peers
    body = comps // 16 * 16
    height = body + TAIL
    groups = levels * xcells
    count = len(stages_of(body))
    lines = row_count // 128

    vmem = pl.BlockSpec(memory_space=pltpu.VMEM)
    anywhere = pl.BlockSpec(memory_space=pl.ANY)
    packed, tails = pl.pallas_call(
        functools.partial(pack_kernel, peers, capacity),
        out_shape=(
            jax.ShapeDtypeStruct((peers, body, capacity), jnp.bfloat16),
            jax.ShapeDtypeStruct((peers, TAIL, capacity // 2), jnp.bfloat16),
        ),
        in_specs=[anywhere, vmem, vmem],
        out_specs=(anywhere, anywhere),
        scratch_shapes=[
            pltpu.VMEM((peers, height, capacity + 512), jnp.bfloat16),
            pltpu.VMEM((peers, TAIL, capacity // 2), jnp.bfloat16),
            pltpu.VMEM((comps, row_count), jnp.bfloat16),
            pltpu.VMEM((lines, 128), jnp.int32),
            pltpu.VMEM((lines, 128), jnp.int32),
            pltpu.SMEM((lines, 128), jnp.int32),
            pltpu.VMEM((8, 128), jnp.int32),
            pltpu.SMEM((8, 128), jnp.int32),
            pltpu.SemaphoreType.DMA,
            pltpu.SemaphoreType.DMA((peers + 2,)),
        ],
        compiler_params=pltpu.CompilerParams(vmem_limit_bytes=48 * 2**20),
        name="pack_rows",
    )(increments, dest_tile.reshape(lines, 128), dest_cell.reshape(lines, 128))

    base = jnp.transpose(base_field, (1, 2, 0, 3)).reshape(groups, comps, ycells)
    settled = pl.pallas_call(
        functools.partial(main_kernel, comps, 1),
        out_shape=jax.ShapeDtypeStruct((groups, comps, ycells), jnp.bfloat16),
        in_specs=[anywhere] * 3 + [vmem] * 3,
        out_specs=vmem,
        scratch_shapes=[
            pltpu.VMEM((peers, body, capacity), jnp.bfloat16),
            pltpu.VMEM((peers, TAIL, capacity // 2), jnp.bfloat16),
            pltpu.VMEM((peers, 8, capacity), jnp.float32),
            pltpu.VMEM((groups, comps, ycells), jnp.bfloat16),
            pltpu.VMEM((groups, height, ycells), jnp.float32),
            pltpu.VMEM((xcells, levels, height, ycells), jnp.bfloat16),
            pltpu.VMEM((xcells, levels, height, ycells), jnp.bfloat16),
            pltpu.VMEM((levels, height, ycells), jnp.bfloat16),
            pltpu.VMEM((levels, height, ycells), jnp.bfloat16),
            pltpu.VMEM((levels, ycells), jnp.float32),
            pltpu.VMEM((xcells, height, ycells), jnp.bfloat16),
            pltpu.VMEM((slabs - 1, xcells, height, ycells), jnp.bfloat16),
            pltpu.VMEM((xcells, height, ycells), jnp.float32),
            pltpu.VMEM((levels, height, 128), jnp.float32),
            pltpu.VMEM((levels, height, 128), jnp.float32),
            pltpu.VMEM((slabs - 1, height, 128), jnp.float32),
            pltpu.VMEM((5, xcells, levels, ycells), jnp.float32),
            pltpu.VMEM((xcells, levels, ycells), jnp.float32),
            pltpu.VMEM((xcells, levels, ycells), jnp.float32),
            pltpu.SemaphoreType.DMA((count, peers)),
            pltpu.SemaphoreType.DMA((count, peers)),
            pltpu.SemaphoreType.DMA((count, 2)),
            pltpu.SemaphoreType.DMA((count, 2)),
            pltpu.SemaphoreType.DMA,
            pltpu.SemaphoreType.DMA,
            pltpu.SemaphoreType.DMA((count, slabs - 1)),
            pltpu.SemaphoreType.DMA((count, slabs - 1)),
            pltpu.SemaphoreType.DMA((3,)),
        ],
        compiler_params=pltpu.CompilerParams(
            vmem_limit_bytes=56 * 2**20, collective_id=0, has_side_effects=True
        ),
        name="exchange_advect_settle",
    )(packed, tails, base, courant_x, courant_y, jnp.transpose(fall_courant))
    settled = settled.reshape(levels, xcells, comps, ycells)
    return jnp.transpose(settled, (2, 0, 1, 3))


def solution(mesh):
    in_specs = (
        P(None, "gz", "xy", None),
        P(None, ("xy", "gz")),
        P(("xy", "gz"), None),
        P(("xy", "gz")),
        P("gz", "xy", None),
        P("gz", "xy", None),
        P(),
    )
    out_specs = P(None, "gz", "xy", None)
    return jax.shard_map(
        per_device, mesh=mesh, in_specs=in_specs, out_specs=out_specs, check_vma=False
    )
```

```python
import functools

import jax
import jax.numpy as jnp
from jax import lax
from jax.experimental import pallas as pl
from jax.experimental.pallas import tpu as pltpu
from jax.sharding import PartitionSpec as P

MESH = pl.DeviceIdType.MESH
NT = (((1,), (1,)), ((), ()))
TAIL = 16


def one_hot(condition):
    return jnp.where(condition, 1.0, 0.0).astype(jnp.bfloat16)


def stages_of(body):
    parts = [(body, TAIL)]
    first = 0
    while first < body:
        rows = 16 if first == 0 or body - first < 48 else 32
        parts.append((first, rows))
        first += rows
    return parts


def pack_kernel(
    peers, capacity, inc_in, tiles, cells, main_out, tail_out, packed, tails, inc, places, starts, table, ends,
    totals, sem, out_sem
):
    comps, count = inc.shape
    inc_copy = pltpu.make_async_copy(inc_in, inc, out_sem.at[peers])
    inc_copy.start()
    body = comps // 16 * 16
    height = body + TAIL
    run, width = 128, 256
    lines = count // run
    half = capacity // 2

    def clear(tile, carry):
        packed[tile] = jnp.zeros(packed.shape[1:], packed.dtype)
        return carry

    lax.fori_loop(0, peers, clear, 0)

    ahead = one_hot(
        lax.broadcasted_iota(jnp.int32, (run, run), 0) <= lax.broadcasted_iota(jnp.int32, (run, run), 1)
    )
    every = jnp.ones((run, run), jnp.bfloat16)
    above = one_hot(
        lax.broadcasted_iota(jnp.int32, (lines, lines), 0)
        > lax.broadcasted_iota(jnp.int32, (lines, lines), 1)
    )
    lanes = lax.broadcasted_iota(jnp.int32, (lines, run), 1)
    bundle = min(8, peers)

    def rank(part, carry):
        place, start, end = carry
        for n in range(bundle):
            tile = part * bundle + n
            member = jnp.where(tiles[...] == tile, 1.0, 0.0)
            taken = member.astype(jnp.bfloat16)
            inside = jnp.dot(taken, ahead, preferred_element_type=jnp.float32)
            line = jnp.dot(taken, every, preferred_element_type=jnp.float32).astype(jnp.bfloat16)
            before = jnp.dot(above, line, preferred_element_type=jnp.float32)
            place = place + member * (inside + before - 1.0)
            start = start + jnp.where(lanes == tile, before, 0.0)
            end = end + jnp.where(
                lanes[0:8] == tile, before[lines - 1 : lines] + line[lines - 1 : lines].astype(jnp.float32), 0.0
            )
        return place, start, end

    zero = jnp.zeros((lines, run), jnp.float32)
    place, start, end = lax.fori_loop(0, peers // bundle, rank, (zero, zero, zero[0:8]))
    places[...] = place.astype(jnp.int32) % width
    starts[...] = start.astype(jnp.int32)
    ends[...] = end.astype(jnp.int32)
    copy = pltpu.make_async_copy(starts, table, sem)
    end_copy = pltpu.make_async_copy(ends, totals, out_sem.at[peers + 1])
    copy.start()
    end_copy.start()
    copy.wait()
    end_copy.wait()

    lane = lax.broadcasted_iota(jnp.int32, (16, width), 1)
    inc_copy.wait()

    def line_of(ref, line, much):
        return jnp.concatenate([ref[pl.ds(line + n, 1)] for n in range(much)], axis=1)

    def place_block(line, much):
        size = much * run
        columns = pl.ds(pl.multiple_of(line * run, run), size)
        window = lax.broadcasted_iota(jnp.int32, (width, size), 0)
        sub = lax.broadcasted_iota(jnp.int32, (8, size), 0)
        match = one_hot(window == line_of(places, line, much))
        owner = line_of(tiles, line, much)
        cell = line_of(cells, line, much)
        extra = jnp.concatenate(
            [inc[body:comps, columns].astype(jnp.float32), jnp.zeros((8 - comps + body, size), jnp.float32)],
            axis=0,
        )
        extra = jnp.where(sub == 4, (cell % width).astype(jnp.float32), extra)
        extra = jnp.where(sub == 5, (cell // width).astype(jnp.float32), extra)
        extra = jnp.concatenate([extra, jnp.zeros((8, size), jnp.float32)], axis=0)
        rows = jnp.concatenate([inc[0:body, columns], extra.astype(jnp.bfloat16)], axis=0)

        def place_part(part, inner):
            first = part * bundle
            masked = jnp.concatenate(
                [rows * one_hot(owner == first + n) for n in range(bundle)], axis=0
            )
            moved = lax.dot_general(masked, match, NT, preferred_element_type=jnp.float32)
            for n in range(bundle):
                tile = first + n
                begin = table[line, tile]
                chunk, low = begin // width, begin % width
                value = moved[n * height : (n + 1) * height].astype(jnp.bfloat16)
                now = one_hot(lane >= low)
                later = one_hot(lane < low)
                here = pl.ds(pl.multiple_of(chunk * width, width), width)
                there = pl.ds(pl.multiple_of(chunk * width + width, width), width)
                now = jnp.concatenate([now] * (height // 16), axis=0)
                later = jnp.concatenate([later] * (height // 16), axis=0)
                packed[tile, :, here] += value * now
                packed[tile, :, there] = value * later
            return inner

        if peers == bundle:
            place_part(0, 0)
        else:
            lax.fori_loop(0, peers // bundle, place_part, 0)

    much = 4
    blocks = lines // much

    def most_held(block, most):
        line = block * much
        following = jnp.minimum(line + much, lines - 1)

        def held(tile, most):
            end = jnp.where(block == blocks - 1, totals[0, tile], table[following, tile])
            return jnp.maximum(most, end - table[line, tile])

        return lax.fori_loop(0, peers, held, most, unroll=bundle)

    most = lax.fori_loop(0, blocks, most_held, 0)

    @pl.when(most <= width)
    def _():
        def step(block, carry):
            place_block(block * much, much)
            return carry

        lax.fori_loop(0, blocks, step, 0, unroll=4)

    @pl.when(most > width)
    def _():
        def step(block, carry):
            place_block(block * 2, 2)
            return carry

        lax.fori_loop(0, lines // 2, step, 0)

    def out_copy(tile):
        return pltpu.make_async_copy(
            packed.at[tile, 0:body, 0:capacity], main_out.at[tile], out_sem.at[tile]
        )

    def leave(tile, carry):
        out_copy(tile).start()
        left = packed[tile, body:height, 0:half].astype(jnp.float32)[0:8]
        right = packed[tile, body:height, half:capacity].astype(jnp.float32)[0:8]
        tails[tile] = jnp.concatenate([left, right], axis=0).astype(jnp.bfloat16)
        return carry

    lax.fori_loop(0, peers, leave, 0)
    copy = pltpu.make_async_copy(tails, tail_out, sem)
    copy.start()

    def left_all(tile, carry):
        out_copy(tile).wait()
        return carry

    lax.fori_loop(0, peers, left_all, 0)
    copy.wait()


def main_kernel(
    comps, ahead, packed, tails, base_in, courant_x, courant_y, fall_in, out, arrived, arrived_tail, cell_of, base, lifted, total,
    updated, advected, left, right, next_cx, flow, inflow, entry, scale, gain, weight, face, cx, cy, send_sem, recv_sem,
    halo_send, halo_recv, face_send, face_recv, flow_send, flow_recv, own_sem,
):
    peers, body, capacity = packed.shape
    xcells, levels, height, width = updated.shape
    slabs = lax.axis_size("gz")
    me, slab = lax.axis_index("xy"), lax.axis_index("gz")
    has_prev, has_next = me > 0, me < peers - 1
    groups = xcells * levels
    stages = stages_of(body)
    half = capacity // 2

    own_main = pltpu.make_async_copy(packed.at[me], arrived.at[0], own_sem.at[0])
    own_tail = pltpu.make_async_copy(tails.at[me], arrived_tail.at[0], own_sem.at[1])
    base_copy = pltpu.make_async_copy(base_in, base, own_sem.at[2])
    own_tail.start()
    own_main.start()
    base_copy.start()

    inner = (lax.broadcasted_iota(jnp.int32, (1, width), 1) > 0).astype(jnp.float32)
    for k in range(levels):
        along_x, along_y = courant_x[k].astype(jnp.float32), courant_y[k].astype(jnp.float32)
        for i in range(xcells):
            row = along_x[i : i + 1]
            cx[i, k : k + 1] = jnp.where(has_prev, row, 0.0) if i == 0 else row
            cy[i, k : k + 1] = along_y[i : i + 1] * inner

    barrier = pltpu.get_barrier_semaphore()

    def greet(step, carry):
        pl.semaphore_signal(
            barrier, inc=1, device_id=((me + step) % peers, slab), device_id_type=MESH
        )
        return carry

    lax.fori_loop(1, peers, greet, 0)
    for step in range(1, slabs):
        pl.semaphore_signal(
            barrier, inc=1, device_id=(me, (slab + step) % slabs), device_id_type=MESH
        )
    pl.semaphore_wait(barrier, peers - 1 + slabs - 1)

    def row_copy(number, step):
        first, rows = stages[number]
        target = (me + step) % peers
        if number == 0:
            source, landing = tails.at[target], arrived_tail.at[step]
        else:
            source = packed.at[target, pl.ds(first, rows)]
            landing = arrived.at[step, pl.ds(first, rows)]
        return pltpu.make_async_remote_copy(
            src_ref=source,
            dst_ref=landing,
            send_sem=send_sem.at[number, step],
            recv_sem=recv_sem.at[number, step],
            device_id=(target, slab),
            device_id_type=MESH,
        )

    def turn(order):
        away = order // 2
        return jnp.where(order % 2 == 0, peers // 2 + away, peers // 2 - 1 - away)

    def start_rows(number):
        def start(order, carry):
            row_copy(number, turn(order)).start()
            return carry

        lax.fori_loop(0, peers - 1, start, 0)

    for number in range(min(ahead, len(stages))):
        start_rows(number)

    face_to_prev = pltpu.make_async_remote_copy(
        src_ref=cx.at[0],
        dst_ref=next_cx,
        send_sem=face_send,
        recv_sem=face_recv,
        device_id=((me + peers - 1) % peers, slab),
        device_id_type=MESH,
    )

    @pl.when(has_prev)
    def _():
        face_to_prev.start()

    @pl.when(jnp.logical_not(has_prev))
    def _():
        left[...] = jnp.zeros_like(left)

    @pl.when(jnp.logical_not(has_next))
    def _():
        right[...] = jnp.zeros_like(right)
        next_cx[...] = jnp.zeros_like(next_cx)

    fall = jnp.transpose(fall_in[...])
    column = lax.broadcasted_iota(jnp.int32, (1, fall.shape[1]), 1)

    def along(values, at):
        picked = jnp.sum(jnp.where(column == at, values, 0.0), axis=1, keepdims=True)
        return jnp.broadcast_to(picked, (values.shape[0], 128))

    for first, rows, filled in ((0, body, body), (body, TAIL, comps - body)):
        rates = fall[first : first + filled]
        if filled < rows:
            rates = jnp.concatenate([rates, jnp.zeros((8 - filled, fall.shape[1]), jnp.float32)], axis=0)
            spare = jnp.zeros((rows - 8, 128), jnp.float32)
        divided = 1.0 / (1.0 + rates)
        kept = rates / (1.0 + rates)

        def put(ref, at, value):
            if filled < rows:
                value = jnp.concatenate([value, spare], axis=0)
            ref[at, first : first + rows] = value

        def coefficients(k, carry):
            put(scale, k, along(divided, slab * levels + k))
            put(gain, k, along(kept, slab * levels + k))
            return carry

        lax.fori_loop(0, levels, coefficients, 0)
        passed = jnp.ones((kept.shape[0], 128), jnp.float32)
        put(weight, 0, passed)
        for d in range(1, slabs - 1):

            def through(k, value):
                return value * along(kept, (slab + d) * levels + k)

            passed = lax.fori_loop(0, levels, through, passed)
            put(weight, d, passed)

    lane_cells = lax.broadcasted_iota(jnp.int32, (width, capacity), 0).astype(jnp.float32)

    def wide(value):
        return jnp.concatenate([value] * (width // 128), axis=1)

    def lift(number):
        first, rows = stages[number]
        filled = min(comps, first + rows) - first

        def component(b, carry):
            for k in range(levels):
                value = base[first + b, k].astype(jnp.float32)
                for part in range(width // 128):
                    lifted[part, pl.ds(k * xcells * rows + b, xcells, stride=rows)] = value[
                        :, part * 128 : (part + 1) * 128
                    ]
            return carry

        lax.fori_loop(0, filled, component, 0)

    def lifted_at(at, rows):
        return jnp.concatenate([lifted[part, pl.ds(at, rows)] for part in range(width // 128)], axis=1)

    def add_rows(number, step, begin):
        first, rows = stages[number]
        bundle = min(groups, 1024 // rows)
        if number == 0:
            block = arrived_tail[step].astype(jnp.float32)
            block = jnp.concatenate([block[0:8], block[8:16]], axis=1)
            cell_of[step] = block
            block = jnp.concatenate([block, jnp.zeros_like(block)], axis=0).astype(jnp.bfloat16)
        else:
            block = arrived[step, first : first + rows]
        low = cell_of[step, 4:5]
        high = cell_of[step, 5:6]
        match = one_hot(lane_cells == low)

        def product(part, inner):
            at = part * bundle
            masked = jnp.concatenate(
                [block * one_hot(high == (at + n).astype(jnp.float32)) for n in range(bundle)], axis=0
            )
            sums = lax.dot_general(masked, match, NT, preferred_element_type=jnp.float32)
            sums = sums.reshape(bundle, rows, width)
            if begin and number > 0:
                for n in range(bundle):
                    spot = pl.multiple_of((at + n) * rows, rows)
                    total[at + n, first : first + rows] = sums[n] + lifted_at(spot, rows)
            elif begin:
                total[pl.ds(at, bundle), first : first + rows] = sums
            else:
                total[pl.ds(at, bundle), first : first + rows] += sums
            return inner

        lax.fori_loop(0, groups // bundle, product, 0)

    def halo_copy(number, which):
        first, rows = stages[number]
        source = updated.at[xcells - 1 if which == 0 else 0, :, pl.ds(first, rows)]
        landing = (left if which == 0 else right).at[:, pl.ds(first, rows)]
        return pltpu.make_async_remote_copy(
            src_ref=source,
            dst_ref=landing,
            send_sem=halo_send.at[number, which],
            recv_sem=halo_recv.at[number, which],
            device_id=((me + (1 if which == 0 else peers - 1)) % peers, slab),
            device_id_type=MESH,
        )

    def finish(number):
        first, rows = stages[number]
        span = slice(first, first + rows)

        def group(counter, carry):
            value = total[counter, span]
            if number == 0:
                value = jnp.concatenate(
                    [
                        value[: comps - body]
                        + lifted_at(pl.multiple_of(counter * rows, rows), 8)[: comps - body],
                        jnp.zeros((rows - comps + body, width), jnp.float32),
                    ],
                    axis=0,
                )
            updated[counter % xcells, counter // xcells, span] = value.astype(jnp.bfloat16)
            return carry

        lax.fori_loop(0, groups, group, 0, unroll=4)

        @pl.when(has_next)
        def _():
            halo_copy(number, 0).start()

        @pl.when(has_prev)
        def _():
            halo_copy(number, 1).start()

    def flow_copy(number, d):
        first, rows = stages[number]
        return pltpu.make_async_remote_copy(
            src_ref=flow.at[:, pl.ds(first, rows)],
            dst_ref=inflow.at[d - 1, :, pl.ds(first, rows)],
            send_sem=flow_send.at[number, d - 1],
            recv_sem=flow_recv.at[number, d - 1],
            device_id=(me, (slab + slabs - d) % slabs),
            device_id_type=MESH,
        )

    def faces():
        @pl.when(has_next)
        def _():
            face_to_prev.wait_recv()

        for i in range(xcells):
            west, south = cx[i], cy[i]
            east = next_cx[...] if i == xcells - 1 else cx[i + 1]
            north = pltpu.roll(south, width - 1, 1)
            face[0, i] = (
                1.0
                - (jnp.maximum(east, 0.0) - jnp.minimum(west, 0.0))
                - (jnp.maximum(north, 0.0) - jnp.minimum(south, 0.0))
            )
            face[1, i] = jnp.maximum(west, 0.0)
            face[2, i] = -jnp.minimum(east, 0.0)
            face[3, i] = jnp.maximum(south, 0.0)
            face[4, i] = -jnp.minimum(north, 0.0)

    def spans(number):
        first, rows = stages[number]
        return [slice(at, at + 16) for at in range(first, first + rows, 16)]

    def advect(number):
        def cells(chosen, span):
            def level(counter, flows):
                k = levels - 1 - counter
                row = pl.ds(k, 1)
                wanted = sorted({i + d for i in chosen for d in (-1, 0, 1)})
                layer = {}
                for i in wanted:
                    ref = left[k, span] if i < 0 else right[k, span] if i == xcells else updated[i, k, span]
                    layer[i] = ref.astype(jnp.float32)
                kept = wide(gain[k, span])
                result = []
                for i, flowing in zip(chosen, flows):
                    current = layer[i]
                    value = (
                        current * face[0, i, row]
                        + layer[i - 1] * face[1, i, row]
                        + layer[i + 1] * face[2, i, row]
                        + pltpu.roll(current, 1, 1) * face[3, i, row]
                        + pltpu.roll(current, width - 1, 1) * face[4, i, row]
                    ).astype(jnp.bfloat16)
                    advected[i, k, span] = value
                    result.append((value.astype(jnp.float32) + flowing) * kept)
                return tuple(result)

            none = tuple(jnp.zeros((16, width), jnp.float32) for _ in chosen)
            flows = lax.fori_loop(0, levels, level, none, unroll=2)
            for i, flowing in zip(chosen, flows):
                flow[i, span] = flowing.astype(jnp.bfloat16)

        inner = list(range(1, xcells - 1))
        for span in spans(number):
            cells(inner, span)

        @pl.when(has_prev)
        def _():
            halo_copy(number, 0).wait_recv()

        @pl.when(has_next)
        def _():
            halo_copy(number, 1).wait_recv()

        for span in spans(number):
            cells([0, xcells - 1], span)
        for d in range(1, slabs):

            @pl.when(slab >= d)
            def _(d=d):
                flow_copy(number, d).start()

    def settle(number):
        @pl.when(slab == slabs - 1)
        def _():
            for i in range(xcells):
                for span in spans(number):
                    entry[i, span] = jnp.zeros((16, width), jnp.float32)

        for d in range(1, slabs):

            @pl.when(slab + d < slabs)
            def _(d=d):
                flow_copy(number, d).wait_recv()
                for i in range(xcells):
                    for span in spans(number):
                        came = inflow[d - 1, i, span].astype(jnp.float32)
                        if d == 1:
                            entry[i, span] = came
                        else:
                            entry[i, span] += wide(weight[d - 1, span]) * came

        for span in spans(number):
            filled = min(comps, span.stop) - span.start

            def level(counter, flows):
                k = levels - 1 - counter
                kept, divided = wide(gain[k, span]), wide(scale[k, span])
                result = []
                for i, flowing in enumerate(flows):
                    value = advected[i, k, span].astype(jnp.float32) + flowing
                    done = (value * divided).astype(jnp.bfloat16)
                    out[k * xcells + i, span.start : span.start + filled] = done[:filled]
                    result.append(value * kept)
                return tuple(result)

            start = tuple(entry[i, span] for i in range(xcells))
            lax.fori_loop(0, levels, level, start, unroll=2)

    own_tail.wait()
    faces()
    for number in range(len(stages)):
        if number + ahead < len(stages):
            start_rows(number + ahead)
        if number == 1:
            own_main.wait()
            base_copy.wait()
            lift(0)
            finish(0)
        if number > 0:
            lift(number)
        add_rows(number, 0, True)

        def receive(order, carry):
            step = turn(order)
            row_copy(number, step).wait_recv()
            add_rows(number, step, False)
            return carry

        middle = (peers - 1) // 2
        lax.fori_loop(0, middle, receive, 0)
        if number > 1:
            settle(number - 2)
        lax.fori_loop(middle, peers - 1, receive, 0)
        if number > 0:
            advect(number - 1)
        if number > 0:
            finish(number)
    settle(len(stages) - 2)
    advect(len(stages) - 1)
    settle(len(stages) - 1)

    for number in range(len(stages)):

        def sent(step, carry):
            row_copy(number, step).wait_send()
            return carry

        lax.fori_loop(1, peers, sent, 0)

        @pl.when(has_next)
        def _():
            halo_copy(number, 0).wait_send()

        @pl.when(has_prev)
        def _():
            halo_copy(number, 1).wait_send()

        for d in range(1, slabs):

            @pl.when(slab >= d)
            def _(d=d):
                flow_copy(number, d).wait_send()

    @pl.when(has_prev)
    def _():
        face_to_prev.wait_send()


def per_device(base_field, increments, dest_tile, dest_cell, courant_x, courant_y, fall_courant):
    comps, levels, xcells, ycells = base_field.shape
    row_count = increments.shape[1]
    peers, slabs = lax.axis_size("xy"), lax.axis_size("gz")
    capacity = 2 * row_count // peers
    body = comps // 16 * 16
    height = body + TAIL
    groups = levels * xcells
    count = len(stages_of(body))
    lines = row_count // 128

    vmem = pl.BlockSpec(memory_space=pltpu.VMEM)
    anywhere = pl.BlockSpec(memory_space=pl.ANY)
    packed, tails = pl.pallas_call(
        functools.partial(pack_kernel, peers, capacity),
        out_shape=(
            jax.ShapeDtypeStruct((peers, body, capacity), jnp.bfloat16),
            jax.ShapeDtypeStruct((peers, TAIL, capacity // 2), jnp.bfloat16),
        ),
        in_specs=[anywhere, vmem, vmem],
        out_specs=(anywhere, anywhere),
        scratch_shapes=[
            pltpu.VMEM((peers, height, capacity + 512), jnp.bfloat16),
            pltpu.VMEM((peers, TAIL, capacity // 2), jnp.bfloat16),
            pltpu.VMEM((comps, row_count), jnp.bfloat16),
            pltpu.VMEM((lines, 128), jnp.int32),
            pltpu.VMEM((lines, 128), jnp.int32),
            pltpu.SMEM((lines, 128), jnp.int32),
            pltpu.VMEM((8, 128), jnp.int32),
            pltpu.SMEM((8, 128), jnp.int32),
            pltpu.SemaphoreType.DMA,
            pltpu.SemaphoreType.DMA((peers + 2,)),
        ],
        compiler_params=pltpu.CompilerParams(vmem_limit_bytes=62 * 2**20),
        name="pack_rows",
    )(increments, dest_tile.reshape(lines, 128), dest_cell.reshape(lines, 128))

    settled = pl.pallas_call(
        functools.partial(main_kernel, comps, 1),
        out_shape=jax.ShapeDtypeStruct((groups, comps, ycells), jnp.bfloat16),
        in_specs=[anywhere] * 3 + [vmem] * 3,
        out_specs=vmem,
        scratch_shapes=[
            pltpu.VMEM((peers, body, capacity), jnp.bfloat16),
            pltpu.VMEM((peers, TAIL, capacity // 2), jnp.bfloat16),
            pltpu.VMEM((peers, 8, capacity), jnp.float32),
            pltpu.VMEM((comps, levels, xcells, ycells), jnp.bfloat16),
            pltpu.VMEM((2, groups * 32, 128), jnp.float32),
            pltpu.VMEM((groups, height, ycells), jnp.float32),
            pltpu.VMEM((xcells, levels, height, ycells), jnp.bfloat16),
            pltpu.VMEM((xcells, levels, height, ycells), jnp.bfloat16),
            pltpu.VMEM((levels, height, ycells), jnp.bfloat16),
            pltpu.VMEM((levels, height, ycells), jnp.bfloat16),
            pltpu.VMEM((levels, ycells), jnp.float32),
            pltpu.VMEM((xcells, height, ycells), jnp.bfloat16),
            pltpu.VMEM((slabs - 1, xcells, height, ycells), jnp.bfloat16),
            pltpu.VMEM((xcells, height, ycells), jnp.float32),
            pltpu.VMEM((levels, height, 128), jnp.float32),
            pltpu.VMEM((levels, height, 128), jnp.float32),
            pltpu.VMEM((slabs - 1, height, 128), jnp.float32),
            pltpu.VMEM((5, xcells, levels, ycells), jnp.float32),
            pltpu.VMEM((xcells, levels, ycells), jnp.float32),
            pltpu.VMEM((xcells, levels, ycells), jnp.float32),
            pltpu.SemaphoreType.DMA((count, peers)),
            pltpu.SemaphoreType.DMA((count, peers)),
            pltpu.SemaphoreType.DMA((count, 2)),
            pltpu.SemaphoreType.DMA((count, 2)),
            pltpu.SemaphoreType.DMA,
            pltpu.SemaphoreType.DMA,
            pltpu.SemaphoreType.DMA((count, slabs - 1)),
            pltpu.SemaphoreType.DMA((count, slabs - 1)),
            pltpu.SemaphoreType.DMA((3,)),
        ],
        compiler_params=pltpu.CompilerParams(
            vmem_limit_bytes=56 * 2**20, collective_id=0, has_side_effects=True
        ),
        name="exchange_advect_settle",
    )(packed, tails, base_field, courant_x, courant_y, jnp.transpose(fall_courant))
    settled = settled.reshape(levels, xcells, comps, ycells)
    return jnp.transpose(settled, (2, 0, 1, 3))


def solution(mesh):
    in_specs = (
        P(None, "gz", "xy", None),
        P(None, ("xy", "gz")),
        P(("xy", "gz"), None),
        P(("xy", "gz")),
        P("gz", "xy", None),
        P("gz", "xy", None),
        P(),
    )
    out_specs = P(None, "gz", "xy", None)
    return jax.shard_map(
        per_device, mesh=mesh, in_specs=in_specs, out_specs=out_specs, check_vma=False
    )
```

```python
import functools

import jax
import jax.numpy as jnp
from jax import lax
from jax.experimental import pallas as pl
from jax.experimental.pallas import tpu as pltpu
from jax.sharding import PartitionSpec as P

MESH = pl.DeviceIdType.MESH
NT = (((1,), (1,)), ((), ()))
TAIL = 16


def one_hot(condition):
    return jnp.where(condition, 1.0, 0.0).astype(jnp.bfloat16)


def stages_of(body):
    parts = [(body, TAIL)]
    first = 0
    while first < body:
        rows = 16 if first == 0 or body - first < 48 else 32
        parts.append((first, rows))
        first += rows
    return parts


def pack_kernel(
    peers, capacity, inc_in, tiles, cells, main_out, tail_out, packed, tails, inc, places, starts, table, ends,
    totals, sem, out_sem
):
    comps, count = inc.shape
    inc_copy = pltpu.make_async_copy(inc_in, inc, out_sem.at[peers])
    inc_copy.start()
    body = comps // 16 * 16
    height = body + TAIL
    run, width = 128, 256
    lines = count // run
    half = capacity // 2

    def clear(tile, carry):
        packed[tile] = jnp.zeros(packed.shape[1:], packed.dtype)
        return carry

    lax.fori_loop(0, peers, clear, 0)

    ahead = one_hot(
        lax.broadcasted_iota(jnp.int32, (run, run), 0) <= lax.broadcasted_iota(jnp.int32, (run, run), 1)
    )
    every = jnp.ones((run, run), jnp.bfloat16)
    above = one_hot(
        lax.broadcasted_iota(jnp.int32, (lines, lines), 0)
        > lax.broadcasted_iota(jnp.int32, (lines, lines), 1)
    )
    lanes = lax.broadcasted_iota(jnp.int32, (lines, run), 1)
    bundle = min(8, peers)

    def rank(part, carry):
        place, start, end = carry
        for n in range(bundle):
            tile = part * bundle + n
            member = jnp.where(tiles[...] == tile, 1.0, 0.0)
            taken = member.astype(jnp.bfloat16)
            inside = jnp.dot(taken, ahead, preferred_element_type=jnp.float32)
            line = jnp.dot(taken, every, preferred_element_type=jnp.float32).astype(jnp.bfloat16)
            before = jnp.dot(above, line, preferred_element_type=jnp.float32)
            place = place + member * (inside + before - 1.0)
            start = start + jnp.where(lanes == tile, before, 0.0)
            end = end + jnp.where(
                lanes[0:8] == tile, before[lines - 1 : lines] + line[lines - 1 : lines].astype(jnp.float32), 0.0
            )
        return place, start, end

    zero = jnp.zeros((lines, run), jnp.float32)
    place, start, end = lax.fori_loop(0, peers // bundle, rank, (zero, zero, zero[0:8]))
    places[...] = place.astype(jnp.int32) % width
    starts[...] = start.astype(jnp.int32)
    ends[...] = end.astype(jnp.int32)
    copy = pltpu.make_async_copy(starts, table, sem)
    end_copy = pltpu.make_async_copy(ends, totals, out_sem.at[peers + 1])
    copy.start()
    end_copy.start()
    copy.wait()
    end_copy.wait()

    lane = lax.broadcasted_iota(jnp.int32, (16, width), 1)
    inc_copy.wait()

    def line_of(ref, line, much):
        return jnp.concatenate([ref[pl.ds(line + n, 1)] for n in range(much)], axis=1)

    def place_block(line, much):
        size = much * run
        columns = pl.ds(pl.multiple_of(line * run, run), size)
        window = lax.broadcasted_iota(jnp.int32, (width, size), 0)
        sub = lax.broadcasted_iota(jnp.int32, (8, size), 0)
        match = one_hot(window == line_of(places, line, much))
        owner = line_of(tiles, line, much)
        cell = line_of(cells, line, much)
        extra = jnp.concatenate(
            [inc[body:comps, columns].astype(jnp.float32), jnp.zeros((8 - comps + body, size), jnp.float32)],
            axis=0,
        )
        extra = jnp.where(sub == 4, (cell % width).astype(jnp.float32), extra)
        extra = jnp.where(sub == 5, (cell // width).astype(jnp.float32), extra)
        extra = jnp.concatenate([extra, jnp.zeros((8, size), jnp.float32)], axis=0)
        rows = jnp.concatenate([inc[0:body, columns], extra.astype(jnp.bfloat16)], axis=0)

        def place_part(part, inner):
            first = part * bundle
            masked = jnp.concatenate(
                [rows * one_hot(owner == first + n) for n in range(bundle)], axis=0
            )
            moved = lax.dot_general(masked, match, NT, preferred_element_type=jnp.float32)
            for n in range(bundle):
                tile = first + n
                begin = table[line, tile]
                chunk, low = begin // width, begin % width
                value = moved[n * height : (n + 1) * height].astype(jnp.bfloat16)
                now = one_hot(lane >= low)
                later = one_hot(lane < low)
                here = pl.ds(pl.multiple_of(chunk * width, width), width)
                there = pl.ds(pl.multiple_of(chunk * width + width, width), width)
                now = jnp.concatenate([now] * (height // 16), axis=0)
                later = jnp.concatenate([later] * (height // 16), axis=0)
                packed[tile, :, here] += value * now
                packed[tile, :, there] = value * later
            return inner

        if peers == bundle:
            place_part(0, 0)
        else:
            lax.fori_loop(0, peers // bundle, place_part, 0)

    much = 4
    blocks = lines // much

    def most_held(block, most):
        line = block * much
        following = jnp.minimum(line + much, lines - 1)

        def held(tile, most):
            end = jnp.where(block == blocks - 1, totals[0, tile], table[following, tile])
            return jnp.maximum(most, end - table[line, tile])

        return lax.fori_loop(0, peers, held, most, unroll=bundle)

    most = lax.fori_loop(0, blocks, most_held, 0)

    @pl.when(most <= width)
    def _():
        def step(block, carry):
            place_block(block * much, much)
            return carry

        lax.fori_loop(0, blocks, step, 0, unroll=4)

    @pl.when(most > width)
    def _():
        def step(block, carry):
            place_block(block * 2, 2)
            return carry

        lax.fori_loop(0, lines // 2, step, 0)

    def out_copy(tile):
        return pltpu.make_async_copy(
            packed.at[tile, 0:body, 0:capacity], main_out.at[tile], out_sem.at[tile]
        )

    def leave(tile, carry):
        out_copy(tile).start()
        left = packed[tile, body:height, 0:half].astype(jnp.float32)[0:8]
        right = packed[tile, body:height, half:capacity].astype(jnp.float32)[0:8]
        tails[tile] = jnp.concatenate([left, right], axis=0).astype(jnp.bfloat16)
        return carry

    lax.fori_loop(0, peers, leave, 0)
    copy = pltpu.make_async_copy(tails, tail_out, sem)
    copy.start()

    def left_all(tile, carry):
        out_copy(tile).wait()
        return carry

    lax.fori_loop(0, peers, left_all, 0)
    copy.wait()


def main_kernel(
    comps, ahead, packed, tails, base_in, courant_x, courant_y, fall_in, out, arrived, arrived_tail, cell_of, base, lifted, total,
    updated, advected, left, right, next_cx, flow, inflow, entry, scale, gain, weight, face, cx, cy, send_sem, recv_sem,
    halo_send, halo_recv, face_send, face_recv, flow_send, flow_recv, own_sem,
):
    peers, body, capacity = packed.shape
    xcells, levels, height, width = updated.shape
    slabs = lax.axis_size("gz")
    me, slab = lax.axis_index("xy"), lax.axis_index("gz")
    has_prev, has_next = me > 0, me < peers - 1
    groups = xcells * levels
    stages = stages_of(body)
    half = capacity // 2

    own_main = pltpu.make_async_copy(packed.at[me], arrived.at[0], own_sem.at[0])
    own_tail = pltpu.make_async_copy(tails.at[me], arrived_tail.at[0], own_sem.at[1])
    base_copy = pltpu.make_async_copy(base_in, base, own_sem.at[2])
    own_tail.start()
    own_main.start()
    base_copy.start()

    inner = (lax.broadcasted_iota(jnp.int32, (1, width), 1) > 0).astype(jnp.float32)
    for k in range(levels):
        along_x, along_y = courant_x[k].astype(jnp.float32), courant_y[k].astype(jnp.float32)
        for i in range(xcells):
            row = along_x[i : i + 1]
            cx[i, k : k + 1] = jnp.where(has_prev, row, 0.0) if i == 0 else row
            cy[i, k : k + 1] = along_y[i : i + 1] * inner

    barrier = pltpu.get_barrier_semaphore()

    def greet(step, carry):
        pl.semaphore_signal(
            barrier, inc=1, device_id=((me + step) % peers, slab), device_id_type=MESH
        )
        return carry

    lax.fori_loop(1, peers, greet, 0)
    for step in range(1, slabs):
        pl.semaphore_signal(
            barrier, inc=1, device_id=(me, (slab + step) % slabs), device_id_type=MESH
        )
    pl.semaphore_wait(barrier, peers - 1 + slabs - 1)

    def row_copy(number, step):
        first, rows = stages[number]
        target = (me + step) % peers
        if number == 0:
            source, landing = tails.at[target], arrived_tail.at[step]
        else:
            source = packed.at[target, pl.ds(first, rows)]
            landing = arrived.at[step, pl.ds(first, rows)]
        return pltpu.make_async_remote_copy(
            src_ref=source,
            dst_ref=landing,
            send_sem=send_sem.at[number, step],
            recv_sem=recv_sem.at[number, step],
            device_id=(target, slab),
            device_id_type=MESH,
        )

    def turn(order):
        away = order // 2
        return jnp.where(order % 2 == 0, peers // 2 + away, peers // 2 - 1 - away)

    def start_rows(number):
        def start(order, carry):
            row_copy(number, turn(order)).start()
            return carry

        lax.fori_loop(0, peers - 1, start, 0)

    for number in range(min(ahead, len(stages))):
        start_rows(number)

    face_to_prev = pltpu.make_async_remote_copy(
        src_ref=cx.at[0],
        dst_ref=next_cx,
        send_sem=face_send,
        recv_sem=face_recv,
        device_id=((me + peers - 1) % peers, slab),
        device_id_type=MESH,
    )

    @pl.when(has_prev)
    def _():
        face_to_prev.start()

    @pl.when(jnp.logical_not(has_prev))
    def _():
        left[...] = jnp.zeros_like(left)

    @pl.when(jnp.logical_not(has_next))
    def _():
        right[...] = jnp.zeros_like(right)
        next_cx[...] = jnp.zeros_like(next_cx)

    fall = jnp.transpose(fall_in[...])
    column = lax.broadcasted_iota(jnp.int32, (1, fall.shape[1]), 1)

    def along(values, at):
        picked = jnp.sum(jnp.where(column == at, values, 0.0), axis=1, keepdims=True)
        return jnp.broadcast_to(picked, (values.shape[0], 128))

    for first, rows, filled in ((0, body, body), (body, TAIL, comps - body)):
        rates = fall[first : first + filled]
        if filled < rows:
            rates = jnp.concatenate([rates, jnp.zeros((8 - filled, fall.shape[1]), jnp.float32)], axis=0)
            spare = jnp.zeros((rows - 8, 128), jnp.float32)
        divided = 1.0 / (1.0 + rates)
        kept = rates / (1.0 + rates)

        def put(ref, at, value):
            if filled < rows:
                value = jnp.concatenate([value, spare], axis=0)
            ref[at, first : first + rows] = value

        def coefficients(k, carry):
            put(scale, k, along(divided, slab * levels + k))
            put(gain, k, along(kept, slab * levels + k))
            return carry

        lax.fori_loop(0, levels, coefficients, 0)
        passed = jnp.ones((kept.shape[0], 128), jnp.float32)
        put(weight, 0, passed)
        for d in range(1, slabs - 1):

            def through(k, value):
                return value * along(kept, (slab + d) * levels + k)

            passed = lax.fori_loop(0, levels, through, passed)
            put(weight, d, passed)

    lane_cells = lax.broadcasted_iota(jnp.int32, (width, capacity), 0).astype(jnp.float32)

    def wide(value):
        return jnp.concatenate([value] * (width // 128), axis=1)

    def lift(number):
        first, rows = stages[number]
        filled = min(comps, first + rows) - first

        def component(b, carry):
            for k in range(levels):
                value = base[first + b, k].astype(jnp.float32)
                for part in range(width // 128):
                    lifted[part, pl.ds(k * xcells * rows + b, xcells, stride=rows)] = value[
                        :, part * 128 : (part + 1) * 128
                    ]
            return carry

        lax.fori_loop(0, filled, component, 0)

    def lifted_at(at, rows):
        return jnp.concatenate([lifted[part, pl.ds(at, rows)] for part in range(width // 128)], axis=1)

    def add_rows(number, step, begin):
        first, rows = stages[number]
        bundle = min(groups, 1024 // rows)
        if number == 0:
            block = arrived_tail[step].astype(jnp.float32)
            block = jnp.concatenate([block[0:8], block[8:16]], axis=1)
            cell_of[step] = block
            block = jnp.concatenate([block, jnp.zeros_like(block)], axis=0).astype(jnp.bfloat16)
        else:
            block = arrived[step, first : first + rows]
        low = cell_of[step, 4:5]
        high = cell_of[step, 5:6]
        match = one_hot(lane_cells == low)

        def product(part, inner):
            at = part * bundle
            masked = jnp.concatenate(
                [block * one_hot(high == (at + n).astype(jnp.float32)) for n in range(bundle)], axis=0
            )
            sums = lax.dot_general(masked, match, NT, preferred_element_type=jnp.float32)
            sums = sums.reshape(bundle, rows, width)
            if begin and number > 0:
                for n in range(bundle):
                    spot = pl.multiple_of((at + n) * rows, rows)
                    total[at + n, first : first + rows] = sums[n] + lifted_at(spot, rows)
            elif begin:
                total[pl.ds(at, bundle), first : first + rows] = sums
            else:
                total[pl.ds(at, bundle), first : first + rows] += sums
            return inner

        lax.fori_loop(0, groups // bundle, product, 0)

    def halo_copy(number, which):
        first, rows = stages[number]
        source = updated.at[xcells - 1 if which == 0 else 0, :, pl.ds(first, rows)]
        landing = (left if which == 0 else right).at[:, pl.ds(first, rows)]
        return pltpu.make_async_remote_copy(
            src_ref=source,
            dst_ref=landing,
            send_sem=halo_send.at[number, which],
            recv_sem=halo_recv.at[number, which],
            device_id=((me + (1 if which == 0 else peers - 1)) % peers, slab),
            device_id_type=MESH,
        )

    def finish(number):
        first, rows = stages[number]
        span = slice(first, first + rows)

        def group(counter, carry):
            value = total[counter, span]
            if number == 0:
                value = jnp.concatenate(
                    [
                        value[: comps - body]
                        + lifted_at(pl.multiple_of(counter * rows, rows), 8)[: comps - body],
                        jnp.zeros((rows - comps + body, width), jnp.float32),
                    ],
                    axis=0,
                )
            updated[counter % xcells, counter // xcells, span] = value.astype(jnp.bfloat16)
            return carry

        lax.fori_loop(0, groups, group, 0, unroll=4)

        @pl.when(has_next)
        def _():
            halo_copy(number, 0).start()

        @pl.when(has_prev)
        def _():
            halo_copy(number, 1).start()

    def flow_copy(number, d):
        first, rows = stages[number]
        return pltpu.make_async_remote_copy(
            src_ref=flow.at[:, pl.ds(first, rows)],
            dst_ref=inflow.at[d - 1, :, pl.ds(first, rows)],
            send_sem=flow_send.at[number, d - 1],
            recv_sem=flow_recv.at[number, d - 1],
            device_id=(me, (slab + slabs - d) % slabs),
            device_id_type=MESH,
        )

    def faces():
        @pl.when(has_next)
        def _():
            face_to_prev.wait_recv()

        for i in range(xcells):
            west, south = cx[i], cy[i]
            east = next_cx[...] if i == xcells - 1 else cx[i + 1]
            north = pltpu.roll(south, width - 1, 1)
            face[0, i] = (
                1.0
                - (jnp.maximum(east, 0.0) - jnp.minimum(west, 0.0))
                - (jnp.maximum(north, 0.0) - jnp.minimum(south, 0.0))
            )
            face[1, i] = jnp.maximum(west, 0.0)
            face[2, i] = -jnp.minimum(east, 0.0)
            face[3, i] = jnp.maximum(south, 0.0)
            face[4, i] = -jnp.minimum(north, 0.0)

    def spans(number):
        first, rows = stages[number]
        return [slice(at, at + 16) for at in range(first, first + rows, 16)]

    def advect(number):
        def cells(chosen, span):
            def level(counter, flows):
                k = levels - 1 - counter
                row = pl.ds(k, 1)
                wanted = sorted({i + d for i in chosen for d in (-1, 0, 1)})
                layer = {}
                for i in wanted:
                    ref = left[k, span] if i < 0 else right[k, span] if i == xcells else updated[i, k, span]
                    layer[i] = ref.astype(jnp.float32)
                kept = wide(gain[k, span])
                result = []
                for i, flowing in zip(chosen, flows):
                    current = layer[i]
                    value = (
                        current * face[0, i, row]
                        + layer[i - 1] * face[1, i, row]
                        + layer[i + 1] * face[2, i, row]
                        + pltpu.roll(current, 1, 1) * face[3, i, row]
                        + pltpu.roll(current, width - 1, 1) * face[4, i, row]
                    ).astype(jnp.bfloat16)
                    advected[i, k, span] = value
                    result.append((value.astype(jnp.float32) + flowing) * kept)
                return tuple(result)

            none = tuple(jnp.zeros((16, width), jnp.float32) for _ in chosen)
            flows = lax.fori_loop(0, levels, level, none, unroll=2)
            for i, flowing in zip(chosen, flows):
                flow[i, span] = flowing.astype(jnp.bfloat16)

        inner = list(range(1, xcells - 1))
        for span in spans(number):
            cells(inner, span)

        @pl.when(has_prev)
        def _():
            halo_copy(number, 0).wait_recv()

        @pl.when(has_next)
        def _():
            halo_copy(number, 1).wait_recv()

        for span in spans(number):
            cells([0, xcells - 1], span)
        for d in range(1, slabs):

            @pl.when(slab >= d)
            def _(d=d):
                flow_copy(number, d).start()

    def settle(number):
        @pl.when(slab == slabs - 1)
        def _():
            for i in range(xcells):
                for span in spans(number):
                    entry[i, span] = jnp.zeros((16, width), jnp.float32)

        for d in range(1, slabs):

            @pl.when(slab + d < slabs)
            def _(d=d):
                flow_copy(number, d).wait_recv()
                for i in range(xcells):
                    for span in spans(number):
                        came = inflow[d - 1, i, span].astype(jnp.float32)
                        if d == 1:
                            entry[i, span] = came
                        else:
                            entry[i, span] += wide(weight[d - 1, span]) * came

        for span in spans(number):
            filled = min(comps, span.stop) - span.start

            def level(counter, flows):
                k = levels - 1 - counter
                kept, divided = wide(gain[k, span]), wide(scale[k, span])
                result = []
                for i, flowing in enumerate(flows):
                    value = advected[i, k, span].astype(jnp.float32) + flowing
                    done = (value * divided).astype(jnp.bfloat16)
                    out[k * xcells + i, span.start : span.start + filled] = done[:filled]
                    result.append(value * kept)
                return tuple(result)

            start = tuple(entry[i, span] for i in range(xcells))
            lax.fori_loop(0, levels, level, start, unroll=2)

    own_tail.wait()
    faces()
    for number in range(len(stages)):
        if number == 1:
            own_main.wait()
            base_copy.wait()
            lift(0)
            finish(0)
        if number > 0:
            lift(number)
        add_rows(number, 0, True)

        def receive(order, carry):
            step = turn(order)
            row_copy(number, step).wait_recv()
            add_rows(number, step, False)
            return carry

        middle = (peers - 1) // 2
        lax.fori_loop(0, 2, receive, 0)
        if number + ahead < len(stages):
            start_rows(number + ahead)
        lax.fori_loop(2, middle, receive, 0)
        if number > 1:
            settle(number - 2)
        lax.fori_loop(middle, peers - 1, receive, 0)
        if number > 0:
            advect(number - 1)
        if number > 0:
            finish(number)
    settle(len(stages) - 2)
    advect(len(stages) - 1)
    settle(len(stages) - 1)

    for number in range(len(stages)):

        def sent(step, carry):
            row_copy(number, step).wait_send()
            return carry

        lax.fori_loop(1, peers, sent, 0)

        @pl.when(has_next)
        def _():
            halo_copy(number, 0).wait_send()

        @pl.when(has_prev)
        def _():
            halo_copy(number, 1).wait_send()

        for d in range(1, slabs):

            @pl.when(slab >= d)
            def _(d=d):
                flow_copy(number, d).wait_send()

    @pl.when(has_prev)
    def _():
        face_to_prev.wait_send()


def per_device(base_field, increments, dest_tile, dest_cell, courant_x, courant_y, fall_courant):
    comps, levels, xcells, ycells = base_field.shape
    row_count = increments.shape[1]
    peers, slabs = lax.axis_size("xy"), lax.axis_size("gz")
    capacity = 2 * row_count // peers
    body = comps // 16 * 16
    height = body + TAIL
    groups = levels * xcells
    count = len(stages_of(body))
    lines = row_count // 128

    vmem = pl.BlockSpec(memory_space=pltpu.VMEM)
    anywhere = pl.BlockSpec(memory_space=pl.ANY)
    packed, tails = pl.pallas_call(
        functools.partial(pack_kernel, peers, capacity),
        out_shape=(
            jax.ShapeDtypeStruct((peers, body, capacity), jnp.bfloat16),
            jax.ShapeDtypeStruct((peers, TAIL, capacity // 2), jnp.bfloat16),
        ),
        in_specs=[anywhere, vmem, vmem],
        out_specs=(anywhere, anywhere),
        scratch_shapes=[
            pltpu.VMEM((peers, height, capacity + 512), jnp.bfloat16),
            pltpu.VMEM((peers, TAIL, capacity // 2), jnp.bfloat16),
            pltpu.VMEM((comps, row_count), jnp.bfloat16),
            pltpu.VMEM((lines, 128), jnp.int32),
            pltpu.VMEM((lines, 128), jnp.int32),
            pltpu.SMEM((lines, 128), jnp.int32),
            pltpu.VMEM((8, 128), jnp.int32),
            pltpu.SMEM((8, 128), jnp.int32),
            pltpu.SemaphoreType.DMA,
            pltpu.SemaphoreType.DMA((peers + 2,)),
        ],
        compiler_params=pltpu.CompilerParams(vmem_limit_bytes=62 * 2**20),
        name="pack_rows",
    )(increments, dest_tile.reshape(lines, 128), dest_cell.reshape(lines, 128))

    settled = pl.pallas_call(
        functools.partial(main_kernel, comps, 1),
        out_shape=jax.ShapeDtypeStruct((groups, comps, ycells), jnp.bfloat16),
        in_specs=[anywhere] * 3 + [vmem] * 3,
        out_specs=vmem,
        scratch_shapes=[
            pltpu.VMEM((peers, body, capacity), jnp.bfloat16),
            pltpu.VMEM((peers, TAIL, capacity // 2), jnp.bfloat16),
            pltpu.VMEM((peers, 8, capacity), jnp.float32),
            pltpu.VMEM((comps, levels, xcells, ycells), jnp.bfloat16),
            pltpu.VMEM((2, groups * 32, 128), jnp.float32),
            pltpu.VMEM((groups, height, ycells), jnp.float32),
            pltpu.VMEM((xcells, levels, height, ycells), jnp.bfloat16),
            pltpu.VMEM((xcells, levels, height, ycells), jnp.bfloat16),
            pltpu.VMEM((levels, height, ycells), jnp.bfloat16),
            pltpu.VMEM((levels, height, ycells), jnp.bfloat16),
            pltpu.VMEM((levels, ycells), jnp.float32),
            pltpu.VMEM((xcells, height, ycells), jnp.bfloat16),
            pltpu.VMEM((slabs - 1, xcells, height, ycells), jnp.bfloat16),
            pltpu.VMEM((xcells, height, ycells), jnp.float32),
            pltpu.VMEM((levels, height, 128), jnp.float32),
            pltpu.VMEM((levels, height, 128), jnp.float32),
            pltpu.VMEM((slabs - 1, height, 128), jnp.float32),
            pltpu.VMEM((5, xcells, levels, ycells), jnp.float32),
            pltpu.VMEM((xcells, levels, ycells), jnp.float32),
            pltpu.VMEM((xcells, levels, ycells), jnp.float32),
            pltpu.SemaphoreType.DMA((count, peers)),
            pltpu.SemaphoreType.DMA((count, peers)),
            pltpu.SemaphoreType.DMA((count, 2)),
            pltpu.SemaphoreType.DMA((count, 2)),
            pltpu.SemaphoreType.DMA,
            pltpu.SemaphoreType.DMA,
            pltpu.SemaphoreType.DMA((count, slabs - 1)),
            pltpu.SemaphoreType.DMA((count, slabs - 1)),
            pltpu.SemaphoreType.DMA((3,)),
        ],
        compiler_params=pltpu.CompilerParams(
            vmem_limit_bytes=56 * 2**20, collective_id=0, has_side_effects=True
        ),
        name="exchange_advect_settle",
    )(packed, tails, base_field, courant_x, courant_y, jnp.transpose(fall_courant))
    settled = settled.reshape(levels, xcells, comps, ycells)
    return jnp.transpose(settled, (2, 0, 1, 3))


def solution(mesh):
    in_specs = (
        P(None, "gz", "xy", None),
        P(None, ("xy", "gz")),
        P(("xy", "gz"), None),
        P(("xy", "gz")),
        P("gz", "xy", None),
        P("gz", "xy", None),
        P(),
    )
    out_specs = P(None, "gz", "xy", None)
    return jax.shard_map(
        per_device, mesh=mesh, in_specs=in_specs, out_specs=out_specs, check_vma=False
    )
```

```python
import functools

import jax
import jax.numpy as jnp
from jax import lax
from jax.experimental import pallas as pl
from jax.experimental.pallas import tpu as pltpu
from jax.sharding import PartitionSpec as P

MESH = pl.DeviceIdType.MESH
NT = (((1,), (1,)), ((), ()))
TAIL = 16


def one_hot(condition):
    return jnp.where(condition, 1.0, 0.0).astype(jnp.bfloat16)


def stages_of(body):
    parts = [(body, TAIL)]
    first = 0
    while first < body:
        rows = 16 if first == 0 or body - first < 48 else 32
        parts.append((first, rows))
        first += rows
    return parts


def pack_kernel(
    peers, capacity, inc_in, tiles, cells, main_out, tail_out, packed, tails, inc, places, starts, table, ends,
    totals, sem, out_sem
):
    comps, count = inc.shape
    inc_copy = pltpu.make_async_copy(inc_in, inc, out_sem.at[peers])
    inc_copy.start()
    body = comps // 16 * 16
    height = body + TAIL
    run, width = 128, 256
    lines = count // run
    half = capacity // 2

    def clear(tile, carry):
        packed[tile] = jnp.zeros(packed.shape[1:], packed.dtype)
        return carry

    lax.fori_loop(0, peers, clear, 0)

    ahead = one_hot(
        lax.broadcasted_iota(jnp.int32, (run, run), 0) <= lax.broadcasted_iota(jnp.int32, (run, run), 1)
    )
    every = jnp.ones((run, run), jnp.bfloat16)
    above = one_hot(
        lax.broadcasted_iota(jnp.int32, (lines, lines), 0)
        > lax.broadcasted_iota(jnp.int32, (lines, lines), 1)
    )
    lanes = lax.broadcasted_iota(jnp.int32, (lines, run), 1)
    bundle = min(8, peers)

    def rank(part, carry):
        place, start, end = carry
        for n in range(bundle):
            tile = part * bundle + n
            member = jnp.where(tiles[...] == tile, 1.0, 0.0)
            taken = member.astype(jnp.bfloat16)
            inside = jnp.dot(taken, ahead, preferred_element_type=jnp.float32)
            line = jnp.dot(taken, every, preferred_element_type=jnp.float32).astype(jnp.bfloat16)
            before = jnp.dot(above, line, preferred_element_type=jnp.float32)
            place = place + member * (inside + before - 1.0)
            start = start + jnp.where(lanes == tile, before, 0.0)
            end = end + jnp.where(
                lanes[0:8] == tile, before[lines - 1 : lines] + line[lines - 1 : lines].astype(jnp.float32), 0.0
            )
        return place, start, end

    zero = jnp.zeros((lines, run), jnp.float32)
    place, start, end = lax.fori_loop(0, peers // bundle, rank, (zero, zero, zero[0:8]))
    places[...] = place.astype(jnp.int32) % width
    starts[...] = start.astype(jnp.int32)
    ends[...] = end.astype(jnp.int32)
    copy = pltpu.make_async_copy(starts, table, sem)
    end_copy = pltpu.make_async_copy(ends, totals, out_sem.at[peers + 1])
    copy.start()
    end_copy.start()
    copy.wait()
    end_copy.wait()

    lane = lax.broadcasted_iota(jnp.int32, (16, width), 1)
    inc_copy.wait()

    def line_of(ref, line, much):
        return jnp.concatenate([ref[pl.ds(line + n, 1)] for n in range(much)], axis=1)

    def place_block(line, much):
        size = much * run
        columns = pl.ds(pl.multiple_of(line * run, run), size)
        window = lax.broadcasted_iota(jnp.int32, (width, size), 0)
        sub = lax.broadcasted_iota(jnp.int32, (8, size), 0)
        match = one_hot(window == line_of(places, line, much))
        owner = line_of(tiles, line, much)
        cell = line_of(cells, line, much)
        extra = jnp.concatenate(
            [inc[body:comps, columns].astype(jnp.float32), jnp.zeros((8 - comps + body, size), jnp.float32)],
            axis=0,
        )
        extra = jnp.where(sub == 4, (cell % width).astype(jnp.float32), extra)
        extra = jnp.where(sub == 5, (cell // width).astype(jnp.float32), extra)
        extra = jnp.concatenate([extra, jnp.zeros((8, size), jnp.float32)], axis=0)
        rows = jnp.concatenate([inc[0:body, columns], extra.astype(jnp.bfloat16)], axis=0)

        def place_part(part, inner):
            first = part * bundle
            masked = jnp.concatenate(
                [rows * one_hot(owner == first + n) for n in range(bundle)], axis=0
            )
            moved = lax.dot_general(masked, match, NT, preferred_element_type=jnp.float32)
            for n in range(bundle):
                tile = first + n
                begin = table[line, tile]
                chunk, low = begin // width, begin % width
                value = moved[n * height : (n + 1) * height].astype(jnp.bfloat16)
                now = one_hot(lane >= low)
                later = one_hot(lane < low)
                here = pl.ds(pl.multiple_of(chunk * width, width), width)
                there = pl.ds(pl.multiple_of(chunk * width + width, width), width)
                now = jnp.concatenate([now] * (height // 16), axis=0)
                later = jnp.concatenate([later] * (height // 16), axis=0)
                packed[tile, :, here] += value * now
                packed[tile, :, there] = value * later
            return inner

        if peers == bundle:
            place_part(0, 0)
        else:
            lax.fori_loop(0, peers // bundle, place_part, 0)

    much = 4
    blocks = lines // much

    def most_held(block, most):
        line = block * much
        following = jnp.minimum(line + much, lines - 1)

        def held(tile, most):
            end = jnp.where(block == blocks - 1, totals[0, tile], table[following, tile])
            return jnp.maximum(most, end - table[line, tile])

        return lax.fori_loop(0, peers, held, most, unroll=bundle)

    most = lax.fori_loop(0, blocks, most_held, 0)

    @pl.when(most <= width)
    def _():
        def step(block, carry):
            place_block(block * much, much)
            return carry

        lax.fori_loop(0, blocks, step, 0, unroll=8)

    @pl.when(most > width)
    def _():
        def step(block, carry):
            place_block(block * 2, 2)
            return carry

        lax.fori_loop(0, lines // 2, step, 0)

    def out_copy(tile):
        return pltpu.make_async_copy(
            packed.at[tile, 0:body, 0:capacity], main_out.at[tile], out_sem.at[tile]
        )

    def leave(tile, carry):
        out_copy(tile).start()
        left = packed[tile, body:height, 0:half].astype(jnp.float32)[0:8]
        right = packed[tile, body:height, half:capacity].astype(jnp.float32)[0:8]
        tails[tile] = jnp.concatenate([left, right], axis=0).astype(jnp.bfloat16)
        return carry

    lax.fori_loop(0, peers, leave, 0)
    copy = pltpu.make_async_copy(tails, tail_out, sem)
    copy.start()

    def left_all(tile, carry):
        out_copy(tile).wait()
        return carry

    lax.fori_loop(0, peers, left_all, 0)
    copy.wait()


def main_kernel(
    comps, ahead, packed, tails, base_in, courant_x, courant_y, fall_in, out, arrived, arrived_tail, cell_of, base, lifted, total,
    updated, advected, left, right, next_cx, flow, inflow, entry, scale, gain, weight, face, cx, cy, send_sem, recv_sem,
    halo_send, halo_recv, face_send, face_recv, flow_send, flow_recv, own_sem,
):
    peers, body, capacity = packed.shape
    xcells, levels, height, width = updated.shape
    slabs = lax.axis_size("gz")
    me, slab = lax.axis_index("xy"), lax.axis_index("gz")
    has_prev, has_next = me > 0, me < peers - 1
    groups = xcells * levels
    stages = stages_of(body)
    half = capacity // 2

    own_main = pltpu.make_async_copy(packed.at[me], arrived.at[0], own_sem.at[0])
    own_tail = pltpu.make_async_copy(tails.at[me], arrived_tail.at[0], own_sem.at[1])
    base_copy = pltpu.make_async_copy(base_in, base, own_sem.at[2])
    own_tail.start()
    own_main.start()
    base_copy.start()

    inner = (lax.broadcasted_iota(jnp.int32, (1, width), 1) > 0).astype(jnp.float32)
    for k in range(levels):
        along_x, along_y = courant_x[k].astype(jnp.float32), courant_y[k].astype(jnp.float32)
        for i in range(xcells):
            row = along_x[i : i + 1]
            cx[i, k : k + 1] = jnp.where(has_prev, row, 0.0) if i == 0 else row
            cy[i, k : k + 1] = along_y[i : i + 1] * inner

    barrier = pltpu.get_barrier_semaphore()

    def greet(step, carry):
        pl.semaphore_signal(
            barrier, inc=1, device_id=((me + step) % peers, slab), device_id_type=MESH
        )
        return carry

    lax.fori_loop(1, peers, greet, 0)
    for step in range(1, slabs):
        pl.semaphore_signal(
            barrier, inc=1, device_id=(me, (slab + step) % slabs), device_id_type=MESH
        )
    pl.semaphore_wait(barrier, peers - 1 + slabs - 1)

    def row_copy(number, step):
        first, rows = stages[number]
        target = (me + step) % peers
        if number == 0:
            source, landing = tails.at[target], arrived_tail.at[step]
        else:
            source = packed.at[target, pl.ds(first, rows)]
            landing = arrived.at[step, pl.ds(first, rows)]
        return pltpu.make_async_remote_copy(
            src_ref=source,
            dst_ref=landing,
            send_sem=send_sem.at[number, step],
            recv_sem=recv_sem.at[number, step],
            device_id=(target, slab),
            device_id_type=MESH,
        )

    def turn(order):
        away = order // 2
        return jnp.where(order % 2 == 0, peers // 2 + away, peers // 2 - 1 - away)

    def start_rows(number):
        def start(order, carry):
            row_copy(number, turn(order)).start()
            return carry

        lax.fori_loop(0, peers - 1, start, 0)

    for number in range(min(ahead, len(stages))):
        start_rows(number)

    face_to_prev = pltpu.make_async_remote_copy(
        src_ref=cx.at[0],
        dst_ref=next_cx,
        send_sem=face_send,
        recv_sem=face_recv,
        device_id=((me + peers - 1) % peers, slab),
        device_id_type=MESH,
    )

    @pl.when(has_prev)
    def _():
        face_to_prev.start()

    @pl.when(jnp.logical_not(has_prev))
    def _():
        left[...] = jnp.zeros_like(left)

    @pl.when(jnp.logical_not(has_next))
    def _():
        right[...] = jnp.zeros_like(right)
        next_cx[...] = jnp.zeros_like(next_cx)

    fall = jnp.transpose(fall_in[...])
    column = lax.broadcasted_iota(jnp.int32, (1, fall.shape[1]), 1)

    def along(values, at):
        picked = jnp.sum(jnp.where(column == at, values, 0.0), axis=1, keepdims=True)
        return jnp.broadcast_to(picked, (values.shape[0], 128))

    for first, rows, filled in ((0, body, body), (body, TAIL, comps - body)):
        rates = fall[first : first + filled]
        if filled < rows:
            rates = jnp.concatenate([rates, jnp.zeros((8 - filled, fall.shape[1]), jnp.float32)], axis=0)
            spare = jnp.zeros((rows - 8, 128), jnp.float32)
        divided = 1.0 / (1.0 + rates)
        kept = rates / (1.0 + rates)

        def put(ref, at, value):
            if filled < rows:
                value = jnp.concatenate([value, spare], axis=0)
            ref[at, first : first + rows] = value

        def coefficients(k, carry):
            put(scale, k, along(divided, slab * levels + k))
            put(gain, k, along(kept, slab * levels + k))
            return carry

        lax.fori_loop(0, levels, coefficients, 0)
        passed = jnp.ones((kept.shape[0], 128), jnp.float32)
        put(weight, 0, passed)
        for d in range(1, slabs - 1):

            def through(k, value):
                return value * along(kept, (slab + d) * levels + k)

            passed = lax.fori_loop(0, levels, through, passed)
            put(weight, d, passed)

    lane_cells = lax.broadcasted_iota(jnp.int32, (width, capacity), 0).astype(jnp.float32)

    def wide(value):
        return jnp.concatenate([value] * (width // 128), axis=1)

    def lift(number):
        first, rows = stages[number]
        filled = min(comps, first + rows) - first

        def component(b, carry):
            for k in range(levels):
                value = base[first + b, k].astype(jnp.float32)
                for part in range(width // 128):
                    lifted[part, pl.ds(k * xcells * rows + b, xcells, stride=rows)] = value[
                        :, part * 128 : (part + 1) * 128
                    ]
            return carry

        lax.fori_loop(0, filled, component, 0)

    def lifted_at(at, rows):
        return jnp.concatenate([lifted[part, pl.ds(at, rows)] for part in range(width // 128)], axis=1)

    def add_rows(number, step, begin):
        first, rows = stages[number]
        bundle = min(groups, 1024 // rows)
        if number == 0:
            block = arrived_tail[step].astype(jnp.float32)
            block = jnp.concatenate([block[0:8], block[8:16]], axis=1)
            cell_of[step] = block
            block = jnp.concatenate([block, jnp.zeros_like(block)], axis=0).astype(jnp.bfloat16)
        else:
            block = arrived[step, first : first + rows]
        low = cell_of[step, 4:5]
        high = cell_of[step, 5:6]
        match = one_hot(lane_cells == low)

        def product(part, inner):
            at = part * bundle
            masked = jnp.concatenate(
                [block * one_hot(high == (at + n).astype(jnp.float32)) for n in range(bundle)], axis=0
            )
            sums = lax.dot_general(masked, match, NT, preferred_element_type=jnp.float32)
            sums = sums.reshape(bundle, rows, width)
            if begin and number > 0:
                for n in range(bundle):
                    spot = pl.multiple_of((at + n) * rows, rows)
                    total[at + n, first : first + rows] = sums[n] + lifted_at(spot, rows)
            elif begin:
                total[pl.ds(at, bundle), first : first + rows] = sums
            else:
                total[pl.ds(at, bundle), first : first + rows] += sums
            return inner

        lax.fori_loop(0, groups // bundle, product, 0)

    def halo_copy(number, which):
        first, rows = stages[number]
        source = updated.at[xcells - 1 if which == 0 else 0, :, pl.ds(first, rows)]
        landing = (left if which == 0 else right).at[:, pl.ds(first, rows)]
        return pltpu.make_async_remote_copy(
            src_ref=source,
            dst_ref=landing,
            send_sem=halo_send.at[number, which],
            recv_sem=halo_recv.at[number, which],
            device_id=((me + (1 if which == 0 else peers - 1)) % peers, slab),
            device_id_type=MESH,
        )

    def finish(number):
        first, rows = stages[number]
        span = slice(first, first + rows)

        def group(counter, carry):
            value = total[counter, span]
            if number == 0:
                value = jnp.concatenate(
                    [
                        value[: comps - body]
                        + lifted_at(pl.multiple_of(counter * rows, rows), 8)[: comps - body],
                        jnp.zeros((rows - comps + body, width), jnp.float32),
                    ],
                    axis=0,
                )
            updated[counter % xcells, counter // xcells, span] = value.astype(jnp.bfloat16)
            return carry

        lax.fori_loop(0, groups, group, 0, unroll=4)

        @pl.when(has_next)
        def _():
            halo_copy(number, 0).start()

        @pl.when(has_prev)
        def _():
            halo_copy(number, 1).start()

    def flow_copy(number, d):
        first, rows = stages[number]
        return pltpu.make_async_remote_copy(
            src_ref=flow.at[:, pl.ds(first, rows)],
            dst_ref=inflow.at[d - 1, :, pl.ds(first, rows)],
            send_sem=flow_send.at[number, d - 1],
            recv_sem=flow_recv.at[number, d - 1],
            device_id=(me, (slab + slabs - d) % slabs),
            device_id_type=MESH,
        )

    def faces():
        @pl.when(has_next)
        def _():
            face_to_prev.wait_recv()

        for i in range(xcells):
            west, south = cx[i], cy[i]
            east = next_cx[...] if i == xcells - 1 else cx[i + 1]
            north = pltpu.roll(south, width - 1, 1)
            face[0, i] = (
                1.0
                - (jnp.maximum(east, 0.0) - jnp.minimum(west, 0.0))
                - (jnp.maximum(north, 0.0) - jnp.minimum(south, 0.0))
            )
            face[1, i] = jnp.maximum(west, 0.0)
            face[2, i] = -jnp.minimum(east, 0.0)
            face[3, i] = jnp.maximum(south, 0.0)
            face[4, i] = -jnp.minimum(north, 0.0)

    def spans(number):
        first, rows = stages[number]
        return [slice(at, at + 16) for at in range(first, first + rows, 16)]

    def advect(number):
        def cells(chosen, span):
            def level(counter, flows):
                k = levels - 1 - counter
                row = pl.ds(k, 1)
                wanted = sorted({i + d for i in chosen for d in (-1, 0, 1)})
                layer = {}
                for i in wanted:
                    ref = left[k, span] if i < 0 else right[k, span] if i == xcells else updated[i, k, span]
                    layer[i] = ref.astype(jnp.float32)
                kept = wide(gain[k, span])
                result = []
                for i, flowing in zip(chosen, flows):
                    current = layer[i]
                    value = (
                        current * face[0, i, row]
                        + layer[i - 1] * face[1, i, row]
                        + layer[i + 1] * face[2, i, row]
                        + pltpu.roll(current, 1, 1) * face[3, i, row]
                        + pltpu.roll(current, width - 1, 1) * face[4, i, row]
                    ).astype(jnp.bfloat16)
                    advected[i, k, span] = value
                    result.append((value.astype(jnp.float32) + flowing) * kept)
                return tuple(result)

            none = tuple(jnp.zeros((16, width), jnp.float32) for _ in chosen)
            flows = lax.fori_loop(0, levels, level, none, unroll=2)
            for i, flowing in zip(chosen, flows):
                flow[i, span] = flowing.astype(jnp.bfloat16)

        inner = list(range(1, xcells - 1))
        for span in spans(number):
            cells(inner, span)

        @pl.when(has_prev)
        def _():
            halo_copy(number, 0).wait_recv()

        @pl.when(has_next)
        def _():
            halo_copy(number, 1).wait_recv()

        for span in spans(number):
            cells([0, xcells - 1], span)
        for d in range(1, slabs):

            @pl.when(slab >= d)
            def _(d=d):
                flow_copy(number, d).start()

    def settle(number):
        @pl.when(slab == slabs - 1)
        def _():
            for i in range(xcells):
                for span in spans(number):
                    entry[i, span] = jnp.zeros((16, width), jnp.float32)

        for d in range(1, slabs):

            @pl.when(slab + d < slabs)
            def _(d=d):
                flow_copy(number, d).wait_recv()
                for i in range(xcells):
                    for span in spans(number):
                        came = inflow[d - 1, i, span].astype(jnp.float32)
                        if d == 1:
                            entry[i, span] = came
                        else:
                            entry[i, span] += wide(weight[d - 1, span]) * came

        for span in spans(number):
            filled = min(comps, span.stop) - span.start

            def level(counter, flows):
                k = levels - 1 - counter
                kept, divided = wide(gain[k, span]), wide(scale[k, span])
                result = []
                for i, flowing in enumerate(flows):
                    value = advected[i, k, span].astype(jnp.float32) + flowing
                    done = (value * divided).astype(jnp.bfloat16)
                    out[k * xcells + i, span.start : span.start + filled] = done[:filled]
                    result.append(value * kept)
                return tuple(result)

            start = tuple(entry[i, span] for i in range(xcells))
            lax.fori_loop(0, levels, level, start, unroll=2)

    own_tail.wait()
    faces()
    for number in range(len(stages)):
        if number == 1:
            own_main.wait()
            base_copy.wait()
            lift(0)
            finish(0)
        if number > 0:
            lift(number)
        add_rows(number, 0, True)

        def receive(order, carry):
            step = turn(order)
            row_copy(number, step).wait_recv()
            add_rows(number, step, False)
            return carry

        middle = (peers - 1) // 2
        lax.fori_loop(0, 2, receive, 0)
        if number + ahead < len(stages):
            start_rows(number + ahead)
        lax.fori_loop(2, middle, receive, 0)
        if number > 1:
            settle(number - 2)
        lax.fori_loop(middle, peers - 1, receive, 0)
        if number > 0:
            advect(number - 1)
        if number > 0:
            finish(number)
    settle(len(stages) - 2)
    advect(len(stages) - 1)
    settle(len(stages) - 1)

    for number in range(len(stages)):

        def sent(step, carry):
            row_copy(number, step).wait_send()
            return carry

        lax.fori_loop(1, peers, sent, 0)

        @pl.when(has_next)
        def _():
            halo_copy(number, 0).wait_send()

        @pl.when(has_prev)
        def _():
            halo_copy(number, 1).wait_send()

        for d in range(1, slabs):

            @pl.when(slab >= d)
            def _(d=d):
                flow_copy(number, d).wait_send()

    @pl.when(has_prev)
    def _():
        face_to_prev.wait_send()


def per_device(base_field, increments, dest_tile, dest_cell, courant_x, courant_y, fall_courant):
    comps, levels, xcells, ycells = base_field.shape
    row_count = increments.shape[1]
    peers, slabs = lax.axis_size("xy"), lax.axis_size("gz")
    capacity = 2 * row_count // peers
    body = comps // 16 * 16
    height = body + TAIL
    groups = levels * xcells
    count = len(stages_of(body))
    lines = row_count // 128

    vmem = pl.BlockSpec(memory_space=pltpu.VMEM)
    anywhere = pl.BlockSpec(memory_space=pl.ANY)
    packed, tails = pl.pallas_call(
        functools.partial(pack_kernel, peers, capacity),
        out_shape=(
            jax.ShapeDtypeStruct((peers, body, capacity), jnp.bfloat16),
            jax.ShapeDtypeStruct((peers, TAIL, capacity // 2), jnp.bfloat16),
        ),
        in_specs=[anywhere, vmem, vmem],
        out_specs=(anywhere, anywhere),
        scratch_shapes=[
            pltpu.VMEM((peers, height, capacity + 512), jnp.bfloat16),
            pltpu.VMEM((peers, TAIL, capacity // 2), jnp.bfloat16),
            pltpu.VMEM((comps, row_count), jnp.bfloat16),
            pltpu.VMEM((lines, 128), jnp.int32),
            pltpu.VMEM((lines, 128), jnp.int32),
            pltpu.SMEM((lines, 128), jnp.int32),
            pltpu.VMEM((8, 128), jnp.int32),
            pltpu.SMEM((8, 128), jnp.int32),
            pltpu.SemaphoreType.DMA,
            pltpu.SemaphoreType.DMA((peers + 2,)),
        ],
        compiler_params=pltpu.CompilerParams(vmem_limit_bytes=62 * 2**20),
        name="pack_rows",
    )(increments, dest_tile.reshape(lines, 128), dest_cell.reshape(lines, 128))

    settled = pl.pallas_call(
        functools.partial(main_kernel, comps, 1),
        out_shape=jax.ShapeDtypeStruct((groups, comps, ycells), jnp.bfloat16),
        in_specs=[anywhere] * 3 + [vmem] * 3,
        out_specs=vmem,
        scratch_shapes=[
            pltpu.VMEM((peers, body, capacity), jnp.bfloat16),
            pltpu.VMEM((peers, TAIL, capacity // 2), jnp.bfloat16),
            pltpu.VMEM((peers, 8, capacity), jnp.float32),
            pltpu.VMEM((comps, levels, xcells, ycells), jnp.bfloat16),
            pltpu.VMEM((2, groups * 32, 128), jnp.float32),
            pltpu.VMEM((groups, height, ycells), jnp.float32),
            pltpu.VMEM((xcells, levels, height, ycells), jnp.bfloat16),
            pltpu.VMEM((xcells, levels, height, ycells), jnp.bfloat16),
            pltpu.VMEM((levels, height, ycells), jnp.bfloat16),
            pltpu.VMEM((levels, height, ycells), jnp.bfloat16),
            pltpu.VMEM((levels, ycells), jnp.float32),
            pltpu.VMEM((xcells, height, ycells), jnp.bfloat16),
            pltpu.VMEM((slabs - 1, xcells, height, ycells), jnp.bfloat16),
            pltpu.VMEM((xcells, height, ycells), jnp.float32),
            pltpu.VMEM((levels, height, 128), jnp.float32),
            pltpu.VMEM((levels, height, 128), jnp.float32),
            pltpu.VMEM((slabs - 1, height, 128), jnp.float32),
            pltpu.VMEM((5, xcells, levels, ycells), jnp.float32),
            pltpu.VMEM((xcells, levels, ycells), jnp.float32),
            pltpu.VMEM((xcells, levels, ycells), jnp.float32),
            pltpu.SemaphoreType.DMA((count, peers)),
            pltpu.SemaphoreType.DMA((count, peers)),
            pltpu.SemaphoreType.DMA((count, 2)),
            pltpu.SemaphoreType.DMA((count, 2)),
            pltpu.SemaphoreType.DMA,
            pltpu.SemaphoreType.DMA,
            pltpu.SemaphoreType.DMA((count, slabs - 1)),
            pltpu.SemaphoreType.DMA((count, slabs - 1)),
            pltpu.SemaphoreType.DMA((3,)),
        ],
        compiler_params=pltpu.CompilerParams(
            vmem_limit_bytes=56 * 2**20, collective_id=0, has_side_effects=True
        ),
        name="exchange_advect_settle",
    )(packed, tails, base_field, courant_x, courant_y, jnp.transpose(fall_courant))
    settled = settled.reshape(levels, xcells, comps, ycells)
    return jnp.transpose(settled, (2, 0, 1, 3))


def solution(mesh):
    in_specs = (
        P(None, "gz", "xy", None),
        P(None, ("xy", "gz")),
        P(("xy", "gz"), None),
        P(("xy", "gz")),
        P("gz", "xy", None),
        P("gz", "xy", None),
        P(),
    )
    out_specs = P(None, "gz", "xy", None)
    return jax.shard_map(
        per_device, mesh=mesh, in_specs=in_specs, out_specs=out_specs, check_vma=False
    )
```
